128 devices in a mesh: tm: 32 (over x, z_lo, y), chan: 4 (over z_hi, core).
Axes of the slice: x: 4, y: 4, z: 4 (z_hi: 2, z_lo: 2; z = z_hi * 2 + z_lo), core: 2. Of those that a mesh axis runs over, the one named last changes fastest.
Arguments:
- launch: float32 [64, 2, 2, 262144], P('chan', None, None, 'tm'), may hold values from -6 to 6
- cotangent: float32 [64, 2, 2, 262144], P('chan', None, None, 'tm'), may hold values from -6 to 6
- filter_taps: float32 [2, 129], replicated, may hold values from -0.375 to 0.375
- offsets: int32 [2, 64], P(None, 'chan'), may hold values from -8 to 8, as said below
Outputs:
- arrival: float32 [64, 2, 2, 262144], P('chan', None, None, 'tm')
- launch_grad: float32 [64, 2, 2, 262144], P('chan', None, None, 'tm')
The draws below stay inside these ranges and needn't reach their ends.
Inputs may be any that keep to these rules, and one draw needn't show every extreme that they name: `offsets`: in every step some channel is walked off by exactly 8 rows forward and some other by exactly 8 rows backward.
All inputs are finite; a program needn't handle non-finite values.
Results may differ from the reference program's by a relative error of at most 0.0001.
Values sent between devices are 32-bit elements; how exact they have to be, the bound alone decides.
A program may use at most 128 MiB of HBM per device.

```python
import jax
import jax.numpy as jnp
from jax import lax

CH = 64
STEPS = 2
MAXOFF = 8
HALF = 64
TIME = 262144


def draw_offsets(key, part):
    key = jax.random.fold_in(key, 7)
    key_base, key_order = jax.random.split(key)
    uniform_rows = jax.random.randint(key_base, (STEPS, CH), -MAXOFF, MAXOFF + 1, dtype=jnp.int32)
    ranking = jax.vmap(lambda single: jax.random.permutation(single, CH))(jax.random.split(key_order, STEPS))
    chosen = jnp.where(ranking == 0, MAXOFF, jnp.where(ranking == 1, -MAXOFF, uniform_rows))
    return chosen.astype(jnp.int32)


def steps_of(stream_key, dims, cuts, low, high):
    loudness, own = 1.0, jax.random.fold_in(stream_key, 6)
    for dim, parts in cuts:
        draws = jnp.exp(jax.random.uniform(jax.random.fold_in(own, dim), (parts,), jnp.float32, low / len(cuts), high / len(cuts)))
        loudness = loudness * jnp.repeat(draws, dims[dim] // parts).reshape([-1 if axis == dim else 1 for axis in range(len(dims))])
    return loudness


def normal_values(own_key, dims, spread, bound, cuts=(), held_as=jnp.bfloat16):
    gain = steps_of(own_key, dims, cuts, -0.22, 0.18) if cuts else 1.0
    drawn = jax.random.normal(own_key, dims, jnp.float32) * spread * gain
    return jnp.minimum(jnp.maximum(drawn, -bound), bound).astype(held_as)


def setup_inputs(seed: int = 0) -> dict:
    streams_of = jax.random.split(jax.random.key(seed), 5)
    launch = normal_values(streams_of[0], (CH, 2, 2, TIME), 1.0, 6.0, ((0, 4), (3, 32)), jnp.float32)
    cotangent = normal_values(streams_of[1], (CH, 2, 2, TIME), 1.0, 6.0, ((0, 4), (3, 32)), jnp.float32)
    filter_taps = normal_values(streams_of[2], (2, 2 * HALF + 1), (4 * HALF + 2) ** -0.5, 0.375, (), jnp.float32)
    offsets = draw_offsets(jax.random.fold_in(streams_of[4], 71), 0)
    return {"launch": launch, "cotangent": cotangent, "filter_taps": filter_taps, "offsets": offsets}


NONLINEAR = 0.001953125

def tap_table(filter_taps):
    span = 2 * HALF + 128
    window_pos = jnp.arange(span)[:, None]
    sample_pos = jnp.arange(128)[None, :]
    tap_index = sample_pos + 2 * HALF - window_pos
    inside = (tap_index >= 0) & (tap_index <= 2 * HALF)
    clipped = jnp.clip(tap_index, 0, 2 * HALF)
    real_part = jnp.where(inside, filter_taps[0][clipped], 0.0)
    imag_part = jnp.where(inside, filter_taps[1][clipped], 0.0)
    upper_rows = jnp.stack([real_part, imag_part], axis=1)
    lower_rows = jnp.stack([-imag_part, real_part], axis=1)
    return jnp.stack([upper_rows, lower_rows], axis=0)

def filter_rows(extended, toeplitz):
    shape_lead = extended.shape[:3]
    row_count = extended.shape[3] // 128 - 1
    gridded = extended.reshape(shape_lead + (row_count + 1, 128))
    windows = jnp.concatenate([gridded[:, :, :, :-1], gridded[:, :, :, 1:]], axis=-1)
    result = jnp.einsum('cpqrj,qjms->cpmrs', windows, toeplitz, precision=lax.Precision.HIGHEST)
    return result.reshape(shape_lead + (row_count * 128,))

def propagate(launch, offsets, toeplitz):
    signal = launch
    for section in range(STEPS):
        shifts = offsets[section] * 128
        moved = jax.vmap(lambda channel_block, offset: jnp.roll(channel_block, offset, axis=-1))(signal, shifts)
        extended = jnp.concatenate([moved[..., -HALF:], moved, moved[..., :HALF]], axis=-1)
        dispersed = filter_rows(extended, toeplitz)
        powers = lax.optimization_barrier(jnp.sum(dispersed * dispersed, axis=(1, 2)))
        totals = lax.optimization_barrier(jnp.sum(powers, axis=0))
        phases = NONLINEAR * (2.0 * totals[None, :] - powers)
        cosine = jnp.cos(phases)[:, None]
        sine_part = jnp.sin(phases)[:, None]
        real_part = dispersed[:, :, 0]
        imag_part = dispersed[:, :, 1]
        signal = jnp.stack([real_part * cosine - imag_part * sine_part, real_part * sine_part + imag_part * cosine], axis=2)
    return signal

def reference(launch, cotangent, filter_taps, offsets):
    toeplitz = tap_table(filter_taps)
    arrival, pullback = jax.vjp(lambda start: propagate(start, offsets, toeplitz), launch)
    gradient = pullback(cotangent)[0]
    return (arrival, gradient)
```

```python
import functools

import jax
import jax.numpy as jnp
from jax import lax
from jax.experimental import pallas as pl
from jax.experimental.pallas import tpu as pltpu
from jax.sharding import PartitionSpec as P

NONLINEAR = 0.001953125
ROWS = 64
HALF = 64
GROUPS = 8
CHANS = 16
MESH = pl.DeviceIdType.MESH
F32 = jnp.float32
BF16 = jnp.bfloat16


def sincos(x):
    k = jnp.floor(x * 0.6366197723675814 + 0.5)
    r = x - k * 1.5703125
    r = r - k * 4.837512969970703125e-4
    r = r - k * 7.549789948768648e-8
    n = k.astype(jnp.int32)
    r2 = r * r
    s = r + r * r2 * (-1.6666654611e-1 + r2 * (8.3321608736e-3 - r2 * 1.9515295891e-4))
    c = 1.0 - 0.5 * r2 + r2 * r2 * (4.166664568298827e-2 + r2 * (2.443315711809948e-5 * r2 - 1.388731625493765e-3))
    swap = (n & 1) == 1
    sine = jnp.where(swap, c, s)
    cosine = jnp.where(swap, s, c)
    sine = jnp.where((n & 2) == 2, -sine, sine)
    cosine = jnp.where(((n + 1) & 2) == 2, -cosine, cosine)
    return cosine, sine


def split(x):
    high = x.astype(BF16)
    low = (x - high.astype(F32)).astype(BF16)
    return high, low


def plane(index, pitch, first):
    return pl.ds(pl.multiple_of(index * pitch, 8) + first, ROWS)


def build_tables(taps, forward, backward):
    row = lax.broadcasted_iota(jnp.int32, (128, 128), 0)
    col = lax.broadcasted_iota(jnp.int32, (128, 128), 1)
    lag = col - row
    mats = []
    for comp in range(2):
        body = jnp.broadcast_to(taps[comp : comp + 1, 0:128], (128, 128))
        last = jnp.broadcast_to(taps[comp : comp + 1, 128:129], (128, 128))
        minus = pltpu.roll(body, HALF, 1)
        plus = jnp.where(col == HALF, last, minus)
        minus = pltpu.roll(minus, 0, 1, stride=1, stride_axis=0)
        plus = pltpu.roll(plus, 0, 1, stride=1, stride_axis=0)
        centre = jnp.where(lag == -HALF, minus, plus)
        centre = jnp.where((lag >= -HALF) & (lag <= HALF), centre, 0.0)
        rim = jnp.where(lag == HALF, minus, plus)
        rim = jnp.where((lag <= -HALF) | (lag >= HALF), rim, 0.0)
        mats.append((centre, rim))
    for table, adjoint in ((forward, False), (backward, True)):
        for part in range(2):
            real, imag = mats[0][part], mats[1][part]
            if adjoint:
                real, imag = real.T, -imag.T
            for place, block in ((0, (real, imag)), (1, (-imag, real))):
                start = part * 256 + place * 128
                for side in range(2):
                    high, low = split(block[side])
                    cols = slice(side * 128, side * 128 + 128)
                    table[start : start + 128, cols] = high
                    table[512 + start : 512 + start + 128, cols] = high
                    table[1024 + start : 1024 + start + 128, cols] = low


def kernel(n, launch, cot, taps, off, arr, grad, X, S, D1, D2, CS1, CS2, C, R, W, LH, PP, TT, TE, TX, RX,
           ES, ER, TF, TB, AST, GST, load_sem, edge_ss, edge_rs, cot_sem, cot_ss, cot_rs, tx_ss, rx_rs,
           w_ss, w_rs, out_sem):
    tm, chan = lax.axis_index("tm"), lax.axis_index("chan")
    nxt, prv = lax.rem(tm + 1, n), lax.rem(tm + n - 1, n)
    core = lax.rem(chan, 2)
    sib = chan + 1 - 2 * core
    far = lax.rem(chan + 2, 4)
    far_sib = lax.rem(sib + 2, 4)

    loads = [
        pltpu.make_async_copy(
            launch.at[pl.ds(4 * g, 4)], X.at[pl.ds(4 * g, 4), pl.ds(8, 128)], load_sem.at[g]
        )
        for g in range(GROUPS)
    ]
    for copy in loads:
        copy.start()
    cot_copy = pltpu.make_async_copy(cot, C.at[:, pl.ds(32, 128)], cot_sem.at[0])
    cot_copy.start()

    barrier = pltpu.get_barrier_semaphore()
    peers = [(tm, sib), (tm, far), (tm, far_sib), (nxt, chan), (nxt, sib), (prv, chan), (prv, sib)]
    for peer in peers:
        pl.semaphore_signal(barrier, inc=1, device_id=peer, device_id_type=MESH)
    pl.semaphore_wait(barrier, len(peers))

    def send(src, dst, ss, rs, peer):
        copy = pltpu.make_async_remote_copy(
            src_ref=src, dst_ref=dst, send_sem=ss, recv_sem=rs, device_id=peer, device_id_type=MESH
        )
        copy.start()
        return copy

    edge_copies = [
        send(launch.at[:, pl.ds(120, 8)], X.at[:, pl.ds(0, 8)], edge_ss.at[0], edge_rs.at[0], (nxt, chan)),
        send(launch.at[:, pl.ds(0, 8)], X.at[:, pl.ds(136, 8)], edge_ss.at[1], edge_rs.at[1], (prv, chan)),
    ]
    cot_copies = [
        send(cot.at[:, pl.ds(96, 32)], C.at[:, pl.ds(0, 32)], cot_ss.at[0], cot_rs.at[0], (nxt, chan)),
        send(cot.at[:, pl.ds(0, 32)], C.at[:, pl.ds(160, 32)], cot_ss.at[1], cot_rs.at[1], (prv, chan)),
    ]

    build_tables(taps, TF, TB)
    PP[...] = jnp.zeros_like(PP)
    lane = lax.broadcasted_iota(jnp.int32, (ROWS, 128), 1)

    def apply_filter(load, table, finish, before=None):
        def body(g, carry):
            if before is not None:
                before(g)
            for j in range(4):
                for comp in range(2):
                    x = load(4 * g + j, comp, 0)
                    z = jnp.where(lane < HALF, load(4 * g + j, comp, 1), load(4 * g + j, comp, -1))
                    for place, value in ((comp, x), (2 + comp, z)):
                        high, low = split(value)
                        LH[j * ROWS : j * ROWS + ROWS, place * 128 : place * 128 + 128] = high
                        LH[j * ROWS : j * ROWS + ROWS, 512 + place * 128 : 640 + place * 128] = low
            operand = jnp.concatenate([LH[...], LH[:, 0:512]], axis=1)
            out = jnp.dot(operand, table[...], preferred_element_type=F32)
            for a in range(2):
                values = []
                for pol in range(2):
                    start = (2 * a + pol) * ROWS
                    values.append((out[start : start + ROWS, 0:128], out[start : start + ROWS, 128:256]))
                finish(2 * g + a, values)
            return carry

        lax.fori_loop(0, GROUPS, body, 0)

    def shift_of(step, c):
        total = off[0, c]
        return total + off[1, c] if step else total

    def exchange_begin(k, step, field):
        reach = 8 * (step + 1)
        margin = reach + 8
        ext = ROWS + 2 * margin
        count = margin + reach

        def add(c, acc):
            return acc + PP[c, pl.ds(40 - margin - shift_of(step, c), ext), :]

        own, own_rows = TX.at[k], TX.at[k, pl.ds(0, ext)]
        ES[k, 0] = field[pl.ds(ROWS - 1, 64, stride=ROWS), :]
        ES[k, 1] = field[pl.ds(0, 64, stride=ROWS), :]
        own[pl.ds(0, ext), :] = lax.fori_loop(0, CHANS, add, jnp.zeros((ext, 128), F32))
        base = 112
        copies = []

        def slot(j, src, dst, peer):
            copies.append(send(src, dst, tx_ss.at[k, j], rx_rs.at[k, j], peer))

        up, down = own.at[pl.ds(64, count)], own.at[pl.ds(8, count)]
        slot(0, own_rows, RX.at[k, pl.ds(0, ext)], (tm, sib))
        slot(1, up, RX.at[k, pl.ds(base, count)], (nxt, chan))
        slot(2, up, RX.at[k, pl.ds(base + 40, count)], (nxt, sib))
        slot(3, down, RX.at[k, pl.ds(base + 80, count)], (prv, chan))
        slot(4, down, RX.at[k, pl.ds(base + 120, count)], (prv, sib))
        slot(5, ES.at[k, 0], ER.at[k, 0], (nxt, chan))
        slot(6, ES.at[k, 1], ER.at[k, 1], (prv, chan))
        return copies

    def exchange_middle(k, step, copies):
        reach = 8 * (step + 1)
        margin = reach + 8
        ext = ROWS + 2 * margin
        count = margin + reach
        base = 112
        for copy in copies[:5]:
            copy.wait()
        pair = TX.at[k, pl.ds(112, 112)]
        pair[pl.ds(0, ext), :] = TX[k, 0:ext] + RX[k, 0:ext]
        pair[pl.ds(0, count), :] = (
            pair[pl.ds(0, count), :] + RX[k, base : base + count] + RX[k, base + 40 : base + 40 + count]
        )
        pair[pl.ds(72, count), :] = (
            pair[pl.ds(72, count), :] + RX[k, base + 80 : base + 80 + count] + RX[k, base + 120 : base + 120 + count]
        )
        half = ext // 2
        src = pair.at[pl.ds(pl.multiple_of(core * half, 8), half)]
        dst = RX.at[k, pl.ds(pl.multiple_of(272 + core * half, 8), half)]
        for j, peer in ((7, (tm, far)), (8, (tm, far_sib))):
            copies.append(send(src, dst, tx_ss.at[k, j], rx_rs.at[k, j], peer))

    def exchange_end(k, step, copies):
        margin = 8 * (step + 1) + 8
        ext = ROWS + 2 * margin
        for copy in copies[7:]:
            copy.wait()
        TT[k, 0:ext] = TX[k, 112 : 112 + ext] + RX[k, 272 : 272 + ext]
        for c in range(CHANS):
            start = margin + shift_of(step, c)
            TE[k, 0, c : c + 1] = TT[k, pl.ds(start - 1, 1), :]
            TE[k, 1, c : c + 1] = TT[k, pl.ds(start + ROWS, 1), :]
        for copy in copies[5:7]:
            copy.wait()
        return margin

    def edge_planes(k, side):
        return [ER.at[k, side][pl.ds(q, CHANS, stride=4), :] for q in range(4)]

    def put_edge(side, planes):
        row = 7 if side == 0 else 72
        for q in range(4):
            S[pl.ds(q * 80 + row, CHANS, stride=320), :] = planes[q]

    for copy in edge_copies:
        copy.wait()

    def load_x(cp, comp, d):
        return X[cp, pl.ds(8 + 2 * d + comp, ROWS, stride=2), :]

    def load_s(cp, comp, d):
        return S[plane(2 * cp + comp, 80, 8 + d), :]

    def keep(store):
        def finish(c, values):
            power = jnp.zeros((ROWS, 128), F32)
            for pol in range(2):
                re, im = values[pol]
                store[plane(4 * c + 2 * pol, ROWS, 0), :] = re
                store[plane(4 * c + 2 * pol + 1, ROWS, 0), :] = im
                power = power + re * re + im * im
            PP[c, 40:104] = power

        return finish

    for copy in loads:
        copy.wait()
    apply_filter(load_x, TF, keep(D1))
    copies = exchange_begin(0, 0, D1)
    exchange_middle(0, 0, copies)
    margin = exchange_end(0, 0, copies)

    def rotate_1(c, carry):
        t = TT[0, pl.ds(16 + shift_of(0, c), ROWS), :]
        cs, sn = sincos(NONLINEAR * (2.0 * t - PP[c, 40:104]))
        CS1[0, c] = cs
        CS1[1, c] = sn
        for pol in range(2):
            re, im = D1[plane(4 * c + 2 * pol, ROWS, 0), :], D1[plane(4 * c + 2 * pol + 1, ROWS, 0), :]
            S[plane(4 * c + 2 * pol, 80, 8), :] = re * cs - im * sn
            S[plane(4 * c + 2 * pol + 1, 80, 8), :] = re * sn + im * cs
        return carry

    lax.fori_loop(0, CHANS, rotate_1, 0)
    for side in range(2):
        e = edge_planes(0, side)
        p = e[0] * e[0] + e[1] * e[1] + e[2] * e[2] + e[3] * e[3]
        cs, sn = sincos(NONLINEAR * (2.0 * TE[0, side] - p))
        put_edge(side, [e[0] * cs - e[1] * sn, e[0] * sn + e[1] * cs, e[2] * cs - e[3] * sn, e[2] * sn + e[3] * cs])

    apply_filter(load_s, TF, keep(D2))
    copies = exchange_begin(1, 1, D2)
    exchange_middle(1, 1, copies)
    cot_copy.wait()
    for copy in cot_copies:
        copy.wait()
    margin = exchange_end(1, 1, copies)

    def rotate_2(c, carry):
        shift = shift_of(1, c)
        t = TT[1, pl.ds(24 + shift, ROWS), :]
        cs, sn = sincos(NONLINEAR * (2.0 * t - PP[c, 40:104]))
        CS2[0, c] = cs
        CS2[1, c] = sn
        q = jnp.zeros((ROWS, 128), F32)
        for pol in range(2):
            re = C[2 * c + pol, pl.ds(32 + 2 * shift, ROWS, stride=2), :]
            im = C[2 * c + pol, pl.ds(33 + 2 * shift, ROWS, stride=2), :]
            rr = re * cs + im * sn
            ri = im * cs - re * sn
            R[plane(4 * c + 2 * pol, ROWS, 0), :] = rr
            R[plane(4 * c + 2 * pol + 1, ROWS, 0), :] = ri
            q = q + ri * D2[plane(4 * c + 2 * pol, ROWS, 0), :] - rr * D2[plane(4 * c + 2 * pol + 1, ROWS, 0), :]
        PP[c, 40:104] = q
        return carry

    lax.fori_loop(0, CHANS, rotate_2, 0)
    copies = exchange_begin(2, 1, R)

    def arrive(c, carry):
        cs, sn = CS2[0, c], CS2[1, c]
        for pol in range(2):
            re, im = D2[plane(4 * c + 2 * pol, ROWS, 0), :], D2[plane(4 * c + 2 * pol + 1, ROWS, 0), :]
            W[4 * c + 2 * pol, 16:80] = re * cs - im * sn
            W[4 * c + 2 * pol + 1, 16:80] = re * sn + im * cs
        return carry

    lax.fori_loop(0, CHANS, arrive, 0)
    exchange_middle(2, 1, copies)
    w_copies = [
        send(W.at[:, pl.ds(64, 16)], W.at[:, pl.ds(0, 16)], w_ss.at[0], w_rs.at[0], (nxt, chan)),
        send(W.at[:, pl.ds(16, 16)], W.at[:, pl.ds(80, 16)], w_ss.at[1], w_rs.at[1], (prv, chan)),
    ]
    exchange_end(2, 1, copies)

    def weigh(k, step, D):
        margin = 8 * (step + 1) + 8

        def body(c, carry):
            t = TT[k, pl.ds(margin + shift_of(step, c), ROWS), :]
            w = 2.0 * NONLINEAR * (2.0 * t - PP[c, 40:104])
            for q in range(4):
                S[plane(4 * c + q, 80, 8), :] = R[plane(4 * c + q, ROWS, 0), :] + w * D[plane(4 * c + q, ROWS, 0), :]
            return carry

        lax.fori_loop(0, CHANS, body, 0)
        for side in range(2):
            r = edge_planes(k, side)
            d = edge_planes(step, side)
            q = r[1] * d[0] - r[0] * d[1] + r[3] * d[2] - r[2] * d[3]
            w = 2.0 * NONLINEAR * (2.0 * TE[k, side] - q)
            put_edge(side, [r[j] + w * d[j] for j in range(4)])

    weigh(2, 1, D2)

    def back_rotate(c, values):
        cs, sn = CS1[0, c], CS1[1, c]
        q = jnp.zeros((ROWS, 128), F32)
        for pol in range(2):
            re, im = values[pol]
            rr = re * cs + im * sn
            ri = im * cs - re * sn
            R[plane(4 * c + 2 * pol, ROWS, 0), :] = rr
            R[plane(4 * c + 2 * pol + 1, ROWS, 0), :] = ri
            q = q + ri * D1[plane(4 * c + 2 * pol, ROWS, 0), :] - rr * D1[plane(4 * c + 2 * pol + 1, ROWS, 0), :]
        PP[c, 40:104] = q

    apply_filter(load_s, TB, back_rotate)
    copies = exchange_begin(3, 0, R)
    exchange_middle(3, 0, copies)
    exchange_end(3, 0, copies)
    weigh(3, 0, D1)

    def put_grad(c, values):
        for pol in range(2):
            for comp in range(2):
                GST[2 * c + pol, pl.ds(comp, ROWS, stride=2), :] = values[pol][comp]

    apply_filter(load_s, TB, put_grad)
    grad_copy = pltpu.make_async_copy(GST, grad, out_sem.at[0])
    grad_copy.start()

    for copy in w_copies:
        copy.wait()

    def put_arrival(c, carry):
        start = 16 - shift_of(1, c)
        for pol in range(2):
            for comp in range(2):
                AST[2 * c + pol, pl.ds(comp, ROWS, stride=2), :] = W[4 * c + 2 * pol + comp, pl.ds(start, ROWS), :]
        return carry

    lax.fori_loop(0, CHANS, put_arrival, 0)
    arr_copy = pltpu.make_async_copy(AST, arr, out_sem.at[1])
    arr_copy.start()
    grad_copy.wait()
    arr_copy.wait()


def rows_of(x):
    return x.reshape(32, 2, ROWS, 128).transpose(0, 2, 1, 3).reshape(32, 2 * ROWS, 128)


def field_of(x):
    return x.reshape(32, ROWS, 2, 128).transpose(0, 2, 1, 3).reshape(16, 2, 2, ROWS * 128)


def solution(mesh):
    n = mesh.shape["tm"]

    def local(launch, cotangent, filter_taps, offsets):
        out = jax.ShapeDtypeStruct((32, 2 * ROWS, 128), F32)
        anywhere = pl.BlockSpec(memory_space=pl.ANY)
        dma = pltpu.SemaphoreType.DMA
        arrival, gradient = pl.pallas_call(
            functools.partial(kernel, n),
            out_shape=(out, out),
            in_specs=[
                anywhere,
                anywhere,
                pl.BlockSpec(memory_space=pltpu.VMEM),
                pl.BlockSpec(memory_space=pltpu.SMEM),
            ],
            out_specs=(anywhere, anywhere),
            scratch_shapes=[
                pltpu.VMEM((32, 144, 128), F32),
                pltpu.VMEM((64 * 80, 128), F32),
                pltpu.VMEM((64 * ROWS, 128), F32),
                pltpu.VMEM((64 * ROWS, 128), F32),
                pltpu.VMEM((2, CHANS, ROWS, 128), F32),
                pltpu.VMEM((2, CHANS, ROWS, 128), F32),
                pltpu.VMEM((32, 192, 128), F32),
                pltpu.VMEM((64 * ROWS, 128), F32),
                pltpu.VMEM((64, 96, 128), F32),
                pltpu.VMEM((4 * ROWS, 1024), BF16),
                pltpu.VMEM((CHANS, 144, 128), F32),
                pltpu.VMEM((4, 112, 128), F32),
                pltpu.VMEM((4, 2, CHANS, 128), F32),
                pltpu.VMEM((4, 224, 128), F32),
                pltpu.VMEM((4, 384, 128), F32),
                pltpu.VMEM((4, 2, 64, 128), F32),
                pltpu.VMEM((4, 2, 64, 128), F32),
                pltpu.VMEM((1536, 256), BF16),
                pltpu.VMEM((1536, 256), BF16),
                pltpu.VMEM((32, 128, 128), F32),
                pltpu.VMEM((32, 128, 128), F32),
                dma((GROUPS,)),
                dma((2,)),
                dma((2,)),
                dma((1,)),
                dma((2,)),
                dma((2,)),
                dma((4, 9)),
                dma((4, 9)),
                dma((2,)),
                dma((2,)),
                dma((2,)),
            ],
            compiler_params=pltpu.CompilerParams(
                collective_id=0, has_side_effects=True, vmem_limit_bytes=56 * 1024 * 1024
            ),
        )(rows_of(launch), rows_of(cotangent), filter_taps, offsets)
        return field_of(arrival), field_of(gradient)

    placed = (P("chan", None, None, "tm"), P("chan", None, None, "tm"), P(), P(None, "chan"))
    return jax.shard_map(
        local,
        mesh=mesh,
        in_specs=placed,
        out_specs=(P("chan", None, None, "tm"), P("chan", None, None, "tm")),
        check_vma=False,
    )
```

```python
import functools

import jax
import jax.numpy as jnp
from jax import lax
from jax.experimental import pallas as pl
from jax.experimental.pallas import tpu as pltpu
from jax.sharding import PartitionSpec as P

NONLINEAR = 0.001953125
ROWS = 64
HALF = 64
GROUPS = 8
EARLY = 4
CHANS = 16
MESH = pl.DeviceIdType.MESH
F32 = jnp.float32
BF16 = jnp.bfloat16


def sincos(x):
    k = jnp.floor(x * 0.6366197723675814 + 0.5)
    r = x - k * 1.5703125
    r = r - k * 4.837512969970703125e-4
    r = r - k * 7.549789948768648e-8
    n = k.astype(jnp.int32)
    r2 = r * r
    s = r + r * r2 * (-1.6666654611e-1 + r2 * (8.3321608736e-3 - r2 * 1.9515295891e-4))
    c = 1.0 - 0.5 * r2 + r2 * r2 * (4.166664568298827e-2 + r2 * (2.443315711809948e-5 * r2 - 1.388731625493765e-3))
    swap = (n & 1) == 1
    sine = jnp.where(swap, c, s)
    cosine = jnp.where(swap, s, c)
    sine = jnp.where((n & 2) == 2, -sine, sine)
    cosine = jnp.where(((n + 1) & 2) == 2, -cosine, cosine)
    return cosine, sine


def split(x):
    high = x.astype(BF16)
    low = (x - high.astype(F32)).astype(BF16)
    return high, low


def plane(index, pitch, first):
    return pl.ds(pl.multiple_of(index * pitch, 8) + first, ROWS)


def build_tables(taps, forward, backward):
    row = lax.broadcasted_iota(jnp.int32, (128, 128), 0)
    col = lax.broadcasted_iota(jnp.int32, (128, 128), 1)
    lag = col - row
    mats = []
    for comp in range(2):
        body = jnp.broadcast_to(taps[comp : comp + 1, 0:128], (128, 128))
        last = jnp.broadcast_to(taps[comp : comp + 1, 128:129], (128, 128))
        minus = pltpu.roll(body, HALF, 1)
        plus = jnp.where(col == HALF, last, minus)
        minus = pltpu.roll(minus, 0, 1, stride=1, stride_axis=0)
        plus = pltpu.roll(plus, 0, 1, stride=1, stride_axis=0)
        centre = jnp.where(lag == -HALF, minus, plus)
        centre = jnp.where((lag >= -HALF) & (lag <= HALF), centre, 0.0)
        rim = jnp.where(lag == HALF, minus, plus)
        rim = jnp.where((lag <= -HALF) | (lag >= HALF), rim, 0.0)
        mats.append((centre, rim))
    for table, adjoint in ((forward, False), (backward, True)):
        for part in range(2):
            real, imag = mats[0][part], mats[1][part]
            if adjoint:
                real, imag = real.T, -imag.T
            for place, block in ((0, (real, imag)), (1, (-imag, real))):
                start = part * 256 + place * 128
                for side in range(2):
                    high, low = split(block[side])
                    cols = slice(side * 128, side * 128 + 128)
                    table[start : start + 128, cols] = high
                    table[512 + start : 512 + start + 128, cols] = high
                    table[1024 + start : 1024 + start + 128, cols] = low


def kernel(n, launch, cot, taps, off, arr, grad, X, S, D1, D2, CA1, SA1, CP1, SP1, C, R, W, LH, PP, ZR, ZI, TH, TE,
           OWN, RXA, RXF, RXM, RXD, HS, TT, ES, ER, XE, EV, OC, TF, TB, AST, GST, load_sem, edge_ss, edge_rs,
           cot_sem, cot_ss, cot_rs, tx_ss, rx_rs, w_ss, w_rs, grad_sem, arr_sem):
    tm, chan = lax.axis_index("tm"), lax.axis_index("chan")
    nxt, prv = lax.rem(tm + 1, n), lax.rem(tm + n - 1, n)
    core = lax.rem(chan, 2)
    sib = chan + 1 - 2 * core
    far = lax.rem(chan + 2, 4)
    far_sib = lax.rem(sib + 2, 4)
    side_tm = core * nxt + (1 - core) * prv

    def launch_load(g):
        return pltpu.make_async_copy(
            launch.at[pl.ds(4 * g, 4)], X.at[pl.ds(4 * g, 4), pl.ds(8, 128)], load_sem.at[g]
        )

    for g in range(GROUPS):
        launch_load(g).start()
    barrier = pltpu.get_barrier_semaphore()
    peers = [(tm, sib), (tm, far), (nxt, chan), (prv, chan), (side_tm, sib), (side_tm, far_sib)]
    for peer in peers:
        pl.semaphore_signal(barrier, inc=1, device_id=peer, device_id_type=MESH)
    cot_copy = pltpu.make_async_copy(cot, C.at[:, pl.ds(32, 128)], cot_sem.at[0])
    cot_copy.start()

    def send(src, dst, ss, rs, peer):
        copy = pltpu.make_async_remote_copy(
            src_ref=src, dst_ref=dst, send_sem=ss, recv_sem=rs, device_id=peer, device_id_type=MESH
        )
        copy.start()
        return copy

    def move_cot(half):
        cps = pl.ds(16 * half, 16)
        return [
            send(cot.at[cps, pl.ds(96, 32)], C.at[cps, pl.ds(0, 32)], cot_ss.at[half, 0], cot_rs.at[half, 0],
                 (nxt, chan)),
            send(cot.at[cps, pl.ds(0, 32)], C.at[cps, pl.ds(160, 32)], cot_ss.at[half, 1], cot_rs.at[half, 1],
                 (prv, chan)),
        ]

    build_tables(taps, TF, TB)
    for buffer in (PP, ZR, ZI):
        for c in range(CHANS):
            buffer[c * 144 : c * 144 + 40] = jnp.zeros((40, 128), F32)
            buffer[c * 144 + 104 : c * 144 + 144] = jnp.zeros((40, 128), F32)
    X[:, 0:8] = jnp.zeros((32, 8, 128), F32)
    X[:, 136:144] = jnp.zeros((32, 8, 128), F32)
    lane = lax.broadcasted_iota(jnp.int32, (ROWS, 128), 1)

    def apply_filter(load, table, finish, first=0, last=GROUPS, before=None):
        def body(g, carry):
            if before is not None:
                before(g)
            for j in range(4):
                for comp in range(2):
                    x = load(4 * g + j, comp, 0)
                    z = jnp.where(lane < HALF, load(4 * g + j, comp, 1), load(4 * g + j, comp, -1))
                    for place, value in ((comp, x), (2 + comp, z)):
                        high, low = split(value)
                        LH[j * ROWS : j * ROWS + ROWS, place * 128 : place * 128 + 128] = high
                        LH[j * ROWS : j * ROWS + ROWS, 512 + place * 128 : 640 + place * 128] = low
            operand = jnp.concatenate([LH[...], LH[:, 0:512]], axis=1)
            out = jnp.dot(operand, table[...], preferred_element_type=F32)
            for a in range(2):
                values = []
                for pol in range(2):
                    start = (2 * a + pol) * ROWS
                    values.append((out[start : start + ROWS, 0:128], out[start : start + ROWS, 128:256]))
                finish(2 * g + a, values)
            return carry

        lax.fori_loop(first, last, body, 0)

    def shift_of(step, c):
        total = off[0, c]
        return total + off[1, c] if step else total

    def sizes(step):
        reach = 8 * (step + 1)
        margin = reach + 8
        ext = ROWS + 2 * margin
        return margin, ext, ext // 2, margin + reach

    def exchange_begin(k, step, sources):
        margin, ext, half, count = sizes(step)
        for a, source in enumerate(sources):
            def add(c, acc, source=source):
                start = pl.multiple_of(c * 144, 8) + 40 - margin - shift_of(step, c)
                return acc + source[pl.ds(start, ext), :]

            OWN[k, a, 0:ext] = lax.fori_loop(0, CHANS, add, jnp.zeros((ext, 128), F32))
        arrays = len(sources)
        theirs = pl.ds(pl.multiple_of((1 - core) * half, 8), half)
        return [
            send(OWN.at[k, pl.ds(0, arrays), theirs], RXA.at[k, pl.ds(0, arrays), pl.ds(0, half)],
                 tx_ss.at[k, 0], rx_rs.at[k, 0], (tm, sib))
        ]

    def exchange_middle(k, step, copies, arrays, fields):
        margin, ext, half, count = sizes(step)
        for e, field in enumerate(fields):
            ES[k, e, 0] = field[pl.ds(ROWS - 1, 64, stride=ROWS), :]
            ES[k, e, 1] = field[pl.ds(0, 64, stride=ROWS), :]
        copies[0].wait_recv()
        mine = pl.ds(pl.multiple_of(core * half, 8), half)
        for a in range(arrays):
            HS[k, a, 0:half] = OWN[k, a, mine, :] + RXA[k, a, 0:half]
        every = pl.ds(0, arrays)
        start = pl.multiple_of(core * (64 - half) + (1 - core) * 8, 8)
        rim = HS.at[k, every, pl.ds(start, count)]
        copies.append(send(rim, RXD.at[k, every, pl.ds(0, count)], tx_ss.at[k, 1], rx_rs.at[k, 1], (side_tm, far_sib)))
        copies.append(send(rim, RXM.at[k, every, pl.ds(0, count)], tx_ss.at[k, 2], rx_rs.at[k, 2], (side_tm, sib)))
        copies.append(
            send(HS.at[k, every, pl.ds(0, half)], RXF.at[k, every, pl.ds(0, half)], tx_ss.at[k, 3], rx_rs.at[k, 3],
                 (tm, far))
        )
        several = pl.ds(0, len(fields))
        copies.append(send(ES.at[k, several, 0], ER.at[k, several, 0], tx_ss.at[k, 5], rx_rs.at[k, 5], (nxt, chan)))
        copies.append(send(ES.at[k, several, 1], ER.at[k, several, 1], tx_ss.at[k, 6], rx_rs.at[k, 6], (prv, chan)))

    def exchange_end(k, step, copies, arrays):
        margin, ext, half, count = sizes(step)
        for copy in copies[1:4]:
            copy.wait_recv()
        base = pl.multiple_of(core * half, 8)
        rim = pl.multiple_of(core * half + core * (half - count), 8)
        for a in range(arrays):
            TT[k, a, pl.ds(base, half), :] = HS[k, a, 0:half] + RXF[k, a, 0:half]
            TT[k, a, pl.ds(rim, count), :] = TT[k, a, pl.ds(rim, count), :] + RXM[k, a, 0:count] + RXD[k, a, 0:count]
        block = TT.at[k, pl.ds(0, arrays), pl.ds(base, half)]
        last = send(block, block, tx_ss.at[k, 4], rx_rs.at[k, 4], (tm, sib))
        last.wait()
        copies[0].wait_send()
        for copy in copies[1:4]:
            copy.wait_send()
        for copy in copies[4:]:
            copy.wait()

    def edge_rows(k, a, source, step):
        margin = sizes(step)[0]
        for c in range(CHANS):
            start = margin + shift_of(step, c)
            TE[k, a, 0, c : c + 1] = source[pl.ds(start - 1, 1), :]
            TE[k, a, 1, c : c + 1] = source[pl.ds(start + ROWS, 1), :]

    def edge_planes(k, e, side):
        return [ER.at[k, e, side][pl.ds(q, CHANS, stride=4), :] for q in range(4)]

    def put_edge(side, planes):
        row = 7 if side == 0 else 72
        for q in range(4):
            S[pl.ds(q * 80 + row, CHANS, stride=320), :] = planes[q]

    def load_x(cp, comp, d):
        return X[cp, pl.ds(8 + 2 * d + comp, ROWS, stride=2), :]

    def load_s(cp, comp, d):
        return S[plane(2 * cp + comp, 80, 8 + d), :]

    def field(ref, c, q):
        return ref[plane(4 * c + q, ROWS, 0), :]

    def rows(ref, c):
        return ref[plane(c, ROWS, 0), :]

    def middle(ref, c):
        return ref[plane(c, 144, 40), :]

    def keep_1(c, values):
        power = jnp.zeros((ROWS, 128), F32)
        for pol in range(2):
            re, im = values[pol]
            D1[plane(4 * c + 2 * pol, ROWS, 0), :] = re
            D1[plane(4 * c + 2 * pol + 1, ROWS, 0), :] = im
            power = power + re * re + im * im
        PP[plane(c, 144, 40), :] = power
        ca, sa = sincos(NONLINEAR * power)
        CA1[plane(c, ROWS, 0), :] = ca
        SA1[plane(c, ROWS, 0), :] = sa

    def wait_load(g):
        launch_load(g).wait()

    apply_filter(load_x, TF, keep_1, 0, EARLY, wait_load)
    pl.semaphore_wait(barrier, len(peers))
    edge_copies = [
        send(launch.at[:, pl.ds(120, 8)], XE.at[0], edge_ss.at[0], edge_rs.at[0], (nxt, chan)),
        send(launch.at[:, pl.ds(0, 8)], XE.at[1], edge_ss.at[1], edge_rs.at[1], (prv, chan)),
    ]
    cot_copies = move_cot(0)
    apply_filter(load_x, TF, keep_1, EARLY, GROUPS, wait_load)
    for copy in edge_copies:
        copy.wait()
    for cp in range(32):
        EV[0, 2 * cp : 2 * cp + 2] = XE[0, cp, 6:8]
        EV[1, 2 * cp : 2 * cp + 2] = XE[1, cp, 0:2]
    short = lax.broadcasted_iota(jnp.int32, (32, 128), 1)
    pieces = []
    for side in range(2):
        inside = short >= HALF if side == 0 else short < HALF
        parts = [jnp.where(inside, EV.at[side][pl.ds(comp, 32, stride=2), :], 0.0) for comp in range(2)]
        high, low = split(jnp.concatenate(parts, axis=1))
        pieces.append(jnp.concatenate([high, low, high], axis=1))
    rim_table = jnp.concatenate([TF[256:512], TF[768:1024], TF[1280:1536]], axis=0)
    added = jnp.dot(jnp.concatenate(pieces, axis=0), rim_table, preferred_element_type=F32)
    OC[0] = added[:, 0:128]
    OC[1] = added[:, 128:256]
    for side in range(2):
        row = 0 if side == 0 else ROWS - 1
        power = jnp.zeros((CHANS, 128), F32)
        for q in range(4):
            place = pl.ds(q * ROWS + row, CHANS, stride=4 * ROWS)
            value = D1[place, :] + OC.at[q % 2][pl.ds(32 * side + q // 2, CHANS, stride=2), :]
            D1[place, :] = value
            power = power + value * value
        PP[pl.ds(40 + row, CHANS, stride=144), :] = power
        ca, sa = sincos(NONLINEAR * power)
        CA1[pl.ds(row, CHANS, stride=ROWS), :] = ca
        SA1[pl.ds(row, CHANS, stride=ROWS), :] = sa

    copies = exchange_begin(0, 0, [PP])
    exchange_middle(0, 0, copies, 1, [D1])
    cot_copies += move_cot(1)
    exchange_end(0, 0, copies, 1)

    def turn(k):
        ext = sizes(k)[1]
        ct, st = sincos(2.0 * NONLINEAR * TT[k, 0, 0:ext])
        TH[k, 0, 0:ext] = ct
        TH[k, 1, 0:ext] = st

    turn(0)
    edge_rows(0, 0, TH.at[0, 0], 0)
    edge_rows(0, 1, TH.at[0, 1], 0)

    def rotate_1(c, carry):
        start = pl.ds(16 + shift_of(0, c), ROWS)
        ct, st = TH[0, 0, start, :], TH[0, 1, start, :]
        ca, sa = rows(CA1, c), rows(SA1, c)
        cs, sn = ct * ca + st * sa, st * ca - ct * sa
        CP1[plane(c, ROWS, 0), :] = cs
        SP1[plane(c, ROWS, 0), :] = sn
        for pol in range(2):
            re, im = field(D1, c, 2 * pol), field(D1, c, 2 * pol + 1)
            S[plane(4 * c + 2 * pol, 80, 8), :] = re * cs - im * sn
            S[plane(4 * c + 2 * pol + 1, 80, 8), :] = re * sn + im * cs
        return carry

    lax.fori_loop(0, CHANS, rotate_1, 0)
    for side in range(2):
        e = edge_planes(0, 0, side)
        ca, sa = sincos(NONLINEAR * (e[0] * e[0] + e[1] * e[1] + e[2] * e[2] + e[3] * e[3]))
        ct, st = TE[0, 0, side], TE[0, 1, side]
        cs, sn = ct * ca + st * sa, st * ca - ct * sa
        put_edge(side, [e[0] * cs - e[1] * sn, e[0] * sn + e[1] * cs, e[2] * cs - e[3] * sn, e[2] * sn + e[3] * cs])

    cot_copy.wait()
    for copy in cot_copies:
        copy.wait()

    def keep_2(c, values):
        power = jnp.zeros((ROWS, 128), F32)
        for pol in range(2):
            re, im = values[pol]
            power = power + re * re + im * im
        PP[plane(c, 144, 40), :] = power
        ca, sa = sincos(NONLINEAR * power)
        shift = shift_of(1, c)
        zr, zi = jnp.zeros((ROWS, 128), F32), jnp.zeros((ROWS, 128), F32)
        for pol in range(2):
            re, im = values[pol]
            D2[plane(4 * c + 2 * pol, ROWS, 0), :] = re
            D2[plane(4 * c + 2 * pol + 1, ROWS, 0), :] = im
            W[4 * c + 2 * pol, 16:80] = re * ca + im * sa
            W[4 * c + 2 * pol + 1, 16:80] = im * ca - re * sa
            gr = C[2 * c + pol, pl.ds(32 + 2 * shift, ROWS, stride=2), :]
            gi = C[2 * c + pol, pl.ds(33 + 2 * shift, ROWS, stride=2), :]
            hr = gr * ca - gi * sa
            hi = gr * sa + gi * ca
            R[plane(4 * c + 2 * pol, ROWS, 0), :] = hr
            R[plane(4 * c + 2 * pol + 1, ROWS, 0), :] = hi
            zr = zr + hr * re + hi * im
            zi = zi + hi * re - hr * im
        ZR[plane(c, 144, 40), :] = zr
        ZI[plane(c, 144, 40), :] = zi

    apply_filter(load_s, TF, keep_2)
    copies = exchange_begin(1, 1, [PP, ZR, ZI])
    exchange_middle(1, 1, copies, 3, [D2, R])
    w_copies = [
        send(W.at[:, pl.ds(64, 16)], W.at[:, pl.ds(0, 16)], w_ss.at[0], w_rs.at[0], (nxt, chan)),
        send(W.at[:, pl.ds(16, 16)], W.at[:, pl.ds(80, 16)], w_ss.at[1], w_rs.at[1], (prv, chan)),
    ]
    exchange_end(1, 1, copies, 3)
    turn(1)
    TT[1, 0] = TT[1, 2] * TH[1, 0] - TT[1, 1] * TH[1, 1]
    edge_rows(1, 0, TH.at[1, 0], 1)
    edge_rows(1, 1, TH.at[1, 1], 1)
    edge_rows(1, 2, TT.at[1, 0], 1)

    def weigh_2(c, carry):
        start = pl.ds(24 + shift_of(1, c), ROWS)
        ct, st, total = TH[1, 0, start, :], TH[1, 1, start, :], TT[1, 0, start, :]
        own = middle(ZI, c) * ct - middle(ZR, c) * st
        w = 2.0 * NONLINEAR * (2.0 * total - own)
        for pol in range(2):
            rr, ri = field(R, c, 2 * pol), field(R, c, 2 * pol + 1)
            S[plane(4 * c + 2 * pol, 80, 8), :] = rr * ct + ri * st + w * field(D2, c, 2 * pol)
            S[plane(4 * c + 2 * pol + 1, 80, 8), :] = ri * ct - rr * st + w * field(D2, c, 2 * pol + 1)
        return carry

    lax.fori_loop(0, CHANS, weigh_2, 0)
    for side in range(2):
        d, r = edge_planes(1, 0, side), edge_planes(1, 1, side)
        ct, st = TE[1, 0, side], TE[1, 1, side]
        rr = [r[0] * ct + r[1] * st, r[1] * ct - r[0] * st, r[2] * ct + r[3] * st, r[3] * ct - r[2] * st]
        own = rr[1] * d[0] - rr[0] * d[1] + rr[3] * d[2] - rr[2] * d[3]
        w = 2.0 * NONLINEAR * (2.0 * TE[1, 2, side] - own)
        put_edge(side, [rr[q] + w * d[q] for q in range(4)])

    def back_rotate(c, values):
        cs, sn = rows(CP1, c), rows(SP1, c)
        own = jnp.zeros((ROWS, 128), F32)
        for pol in range(2):
            re, im = values[pol]
            rr = re * cs + im * sn
            ri = im * cs - re * sn
            R[plane(4 * c + 2 * pol, ROWS, 0), :] = rr
            R[plane(4 * c + 2 * pol + 1, ROWS, 0), :] = ri
            own = own + ri * field(D1, c, 2 * pol) - rr * field(D1, c, 2 * pol + 1)
        PP[plane(c, 144, 40), :] = own

    apply_filter(load_s, TB, back_rotate)
    copies = exchange_begin(2, 0, [PP])
    exchange_middle(2, 0, copies, 1, [R])

    for copy in w_copies:
        copy.wait()

    def put_arrival(c, carry):
        start = pl.ds(16 - shift_of(1, c), ROWS)
        ct, st = TH[1, 0, 24:88], TH[1, 1, 24:88]
        for pol in range(2):
            re, im = W[4 * c + 2 * pol, start, :], W[4 * c + 2 * pol + 1, start, :]
            AST[2 * c + pol, pl.ds(0, ROWS, stride=2), :] = re * ct - im * st
            AST[2 * c + pol, pl.ds(1, ROWS, stride=2), :] = re * st + im * ct
        return carry

    lax.fori_loop(0, CHANS, put_arrival, 0)
    arr_copy = pltpu.make_async_copy(AST, arr, arr_sem.at[0])
    arr_copy.start()
    exchange_end(2, 0, copies, 1)
    edge_rows(2, 0, TT.at[2, 0], 0)

    def weigh_1(c, carry):
        total = TT[2, 0, pl.ds(16 + shift_of(0, c), ROWS), :]
        w = 2.0 * NONLINEAR * (2.0 * total - middle(PP, c))
        for q in range(4):
            S[plane(4 * c + q, 80, 8), :] = field(R, c, q) + w * field(D1, c, q)
        return carry

    lax.fori_loop(0, CHANS, weigh_1, 0)
    for side in range(2):
        r, d = edge_planes(2, 0, side), edge_planes(0, 0, side)
        own = r[1] * d[0] - r[0] * d[1] + r[3] * d[2] - r[2] * d[3]
        w = 2.0 * NONLINEAR * (2.0 * TE[2, 0, side] - own)
        put_edge(side, [r[q] + w * d[q] for q in range(4)])

    def grad_store(g):
        return pltpu.make_async_copy(GST.at[pl.ds(4 * g, 4)], grad.at[pl.ds(4 * g, 4)], grad_sem.at[g])

    def put_grad(c, values):
        for pol in range(2):
            for comp in range(2):
                GST[2 * c + pol, pl.ds(comp, ROWS, stride=2), :] = values[pol][comp]

    def store_previous(g):
        @pl.when(g > 0)
        def _():
            grad_store(g - 1).start()

    apply_filter(load_s, TB, put_grad, 0, GROUPS, store_previous)
    grad_store(GROUPS - 1).start()
    arr_copy.wait()
    for g in range(GROUPS):
        grad_store(g).wait()


def rows_of(x):
    return x.reshape(32, 2, ROWS, 128).transpose(0, 2, 1, 3).reshape(32, 2 * ROWS, 128)


def field_of(x):
    return x.reshape(32, ROWS, 2, 128).transpose(0, 2, 1, 3).reshape(16, 2, 2, ROWS * 128)


def solution(mesh):
    n = mesh.shape["tm"]

    def local(launch, cotangent, filter_taps, offsets):
        out = jax.ShapeDtypeStruct((32, 2 * ROWS, 128), F32)
        anywhere = pl.BlockSpec(memory_space=pl.ANY)
        dma = pltpu.SemaphoreType.DMA
        arrival, gradient = pl.pallas_call(
            functools.partial(kernel, n),
            out_shape=(out, out),
            in_specs=[
                anywhere,
                anywhere,
                pl.BlockSpec(memory_space=pltpu.VMEM),
                pl.BlockSpec(memory_space=pltpu.SMEM),
            ],
            out_specs=(anywhere, anywhere),
            scratch_shapes=[
                pltpu.VMEM((32, 144, 128), F32),
                pltpu.VMEM((64 * 80, 128), F32),
                pltpu.VMEM((64 * ROWS, 128), F32),
                pltpu.VMEM((64 * ROWS, 128), F32),
                pltpu.VMEM((CHANS * ROWS, 128), F32),
                pltpu.VMEM((CHANS * ROWS, 128), F32),
                pltpu.VMEM((CHANS * ROWS, 128), F32),
                pltpu.VMEM((CHANS * ROWS, 128), F32),
                pltpu.VMEM((32, 192, 128), F32),
                pltpu.VMEM((64 * ROWS, 128), F32),
                pltpu.VMEM((64, 96, 128), F32),
                pltpu.VMEM((4 * ROWS, 1024), BF16),
                pltpu.VMEM((CHANS * 144, 128), F32),
                pltpu.VMEM((CHANS * 144, 128), F32),
                pltpu.VMEM((CHANS * 144, 128), F32),
                pltpu.VMEM((2, 2, 112, 128), F32),
                pltpu.VMEM((3, 3, 2, CHANS, 128), F32),
                pltpu.VMEM((3, 3, 112, 128), F32),
                pltpu.VMEM((3, 3, 56, 128), F32),
                pltpu.VMEM((3, 3, 56, 128), F32),
                pltpu.VMEM((3, 3, 40, 128), F32),
                pltpu.VMEM((3, 3, 40, 128), F32),
                pltpu.VMEM((3, 3, 56, 128), F32),
                pltpu.VMEM((3, 3, 112, 128), F32),
                pltpu.VMEM((3, 2, 2, 64, 128), F32),
                pltpu.VMEM((3, 2, 2, 64, 128), F32),
                pltpu.VMEM((2, 32, 8, 128), F32),
                pltpu.VMEM((2, 64, 128), F32),
                pltpu.VMEM((2, 64, 128), F32),
                pltpu.VMEM((1536, 256), BF16),
                pltpu.VMEM((1536, 256), BF16),
                pltpu.VMEM((32, 128, 128), F32),
                pltpu.VMEM((32, 128, 128), F32),
                dma((GROUPS,)),
                dma((2,)),
                dma((2,)),
                dma((1,)),
                dma((2, 2)),
                dma((2, 2)),
                dma((3, 7)),
                dma((3, 7)),
                dma((2,)),
                dma((2,)),
                dma((GROUPS,)),
                dma((1,)),
            ],
            compiler_params=pltpu.CompilerParams(
                collective_id=0, has_side_effects=True, vmem_limit_bytes=56 * 1024 * 1024
            ),
        )(rows_of(launch), rows_of(cotangent), filter_taps, offsets)
        return field_of(arrival), field_of(gradient)

    placed = (P("chan", None, None, "tm"), P("chan", None, None, "tm"), P(), P(None, "chan"))
    return jax.shard_map(
        local,
        mesh=mesh,
        in_specs=placed,
        out_specs=(P("chan", None, None, "tm"), P("chan", None, None, "tm")),
        check_vma=False,
    )
```

```python
import functools

import jax
import jax.numpy as jnp
from jax import lax
from jax.experimental import pallas as pl
from jax.experimental.pallas import tpu as pltpu
from jax.sharding import PartitionSpec as P

NONLINEAR = 0.001953125
ROWS = 64
HALF = 64
GROUPS = 4
EARLY = 2
PLANES = 32 // GROUPS
CHANS = 16
MESH = pl.DeviceIdType.MESH
F32 = jnp.float32
BF16 = jnp.bfloat16


def sincos(x):
    k = jnp.floor(x * 0.6366197723675814 + 0.5)
    r = x - k * 1.5703125
    r = r - k * 4.837512969970703125e-4
    r = r - k * 7.549789948768648e-8
    n = k.astype(jnp.int32)
    r2 = r * r
    s = r + r * r2 * (-1.6666654611e-1 + r2 * (8.3321608736e-3 - r2 * 1.9515295891e-4))
    c = 1.0 - 0.5 * r2 + r2 * r2 * (4.166664568298827e-2 + r2 * (2.443315711809948e-5 * r2 - 1.388731625493765e-3))
    swap = (n & 1) == 1
    sine = jnp.where(swap, c, s)
    cosine = jnp.where(swap, s, c)
    sine = jnp.where((n & 2) == 2, -sine, sine)
    cosine = jnp.where(((n + 1) & 2) == 2, -cosine, cosine)
    return cosine, sine


def split(x):
    high = x.astype(BF16)
    low = (x - high.astype(F32)).astype(BF16)
    return high, low


def plane(index, pitch, first):
    return pl.ds(pl.multiple_of(index * pitch, 8) + first, ROWS)


def build_tables(taps, forward, backward):
    row = lax.broadcasted_iota(jnp.int32, (128, 128), 0)
    col = lax.broadcasted_iota(jnp.int32, (128, 128), 1)
    lag = col - row
    mats = []
    for comp in range(2):
        body = jnp.broadcast_to(taps[comp : comp + 1, 0:128], (128, 128))
        last = jnp.broadcast_to(taps[comp : comp + 1, 128:129], (128, 128))
        minus = pltpu.roll(body, HALF, 1)
        plus = jnp.where(col == HALF, last, minus)
        minus = pltpu.roll(minus, 0, 1, stride=1, stride_axis=0)
        plus = pltpu.roll(plus, 0, 1, stride=1, stride_axis=0)
        centre = jnp.where(lag == -HALF, minus, plus)
        centre = jnp.where((lag >= -HALF) & (lag <= HALF), centre, 0.0)
        rim = jnp.where(lag == HALF, minus, plus)
        rim = jnp.where((lag <= -HALF) | (lag >= HALF), rim, 0.0)
        mats.append((centre, rim))
    for table, adjoint in ((forward, False), (backward, True)):
        for part in range(2):
            real, imag = mats[0][part], mats[1][part]
            if adjoint:
                real, imag = real.T, -imag.T
            for place, block in ((0, (real, imag)), (1, (-imag, real))):
                start = part * 256 + place * 128
                for side in range(2):
                    high, low = split(block[side])
                    cols = slice(side * 128, side * 128 + 128)
                    table[start : start + 128, cols] = high
                    table[512 + start : 512 + start + 128, cols] = high
                    table[1024 + start : 1024 + start + 128, cols] = low


def kernel(n, launch, cot, taps, off, arr, grad, X, S, D1, D2, CA1, SA1, CP1, SP1, CP2, SP2, C, R, W, LHA, LHB, PP, ZR, ZI, TH, TE,
           OWN, RXA, RXF, RXM, RXD, HS, TT, ES, ER, XE, EV, OC, TF, TB, load_sem, edge_ss, edge_rs,
           cot_sem, cot_ss, cot_rs, tx_ss, rx_rs, w_ss, w_rs):
    tm, chan = lax.axis_index("tm"), lax.axis_index("chan")
    nxt, prv = lax.rem(tm + 1, n), lax.rem(tm + n - 1, n)
    core = lax.rem(chan, 2)
    sib = chan + 1 - 2 * core
    far = lax.rem(chan + 2, 4)
    far_sib = lax.rem(sib + 2, 4)
    side_tm = core * nxt + (1 - core) * prv

    def launch_load(g):
        return pltpu.make_async_copy(
            launch.at[pl.ds(PLANES * g, PLANES)], X.at[pl.ds(PLANES * g, PLANES), pl.ds(8, 128)], load_sem.at[g]
        )

    for g in range(GROUPS):
        launch_load(g).start()
    barrier = pltpu.get_barrier_semaphore()
    peers = [(tm, sib), (tm, far), (nxt, chan), (prv, chan), (side_tm, sib), (side_tm, far_sib)]
    for peer in peers:
        pl.semaphore_signal(barrier, inc=1, device_id=peer, device_id_type=MESH)
    cot_copy = pltpu.make_async_copy(cot, C.at[:, pl.ds(32, 128)], cot_sem.at[0])
    cot_copy.start()

    def send(src, dst, ss, rs, peer):
        copy = pltpu.make_async_remote_copy(
            src_ref=src, dst_ref=dst, send_sem=ss, recv_sem=rs, device_id=peer, device_id_type=MESH
        )
        copy.start()
        return copy

    def move_cot(half):
        cps = pl.ds(16 * half, 16)
        return [
            send(cot.at[cps, pl.ds(96, 32)], C.at[cps, pl.ds(0, 32)], cot_ss.at[half, 0], cot_rs.at[half, 0],
                 (nxt, chan)),
            send(cot.at[cps, pl.ds(0, 32)], C.at[cps, pl.ds(160, 32)], cot_ss.at[half, 1], cot_rs.at[half, 1],
                 (prv, chan)),
        ]

    build_tables(taps, TF, TB)
    for buffer in (PP, ZR, ZI):
        for c in range(CHANS):
            buffer[c * 144 : c * 144 + 40] = jnp.zeros((40, 128), F32)
            buffer[c * 144 + 104 : c * 144 + 144] = jnp.zeros((40, 128), F32)
    X[:, 0:8] = jnp.zeros((32, 8, 128), F32)
    X[:, 136:144] = jnp.zeros((32, 8, 128), F32)
    lane = lax.broadcasted_iota(jnp.int32, (ROWS, 128), 1)

    def apply_filter(load, table, finish, first=0, last=GROUPS, before=None):
        def prepare(g, LH):
            for j in range(PLANES):
                for comp in range(2):
                    x = load(PLANES * g + j, comp, 0)
                    z = jnp.where(lane < HALF, load(PLANES * g + j, comp, 1), load(PLANES * g + j, comp, -1))
                    for place, value in ((comp, x), (2 + comp, z)):
                        high, low = split(value)
                        LH[j * ROWS : j * ROWS + ROWS, place * 128 : place * 128 + 128] = high
                        LH[j * ROWS : j * ROWS + ROWS, 512 + place * 128 : 640 + place * 128] = low

        def multiply(LH):
            out = jnp.dot(LH[...], table[0:1024], preferred_element_type=F32)
            return out + jnp.dot(LH[:, 0:512], table[1024:1536], preferred_element_type=F32)

        def complete(g, out):
            for a in range(PLANES // 2):
                values = []
                for pol in range(2):
                    start = (2 * a + pol) * ROWS
                    values.append((out[start : start + ROWS, 0:128], out[start : start + ROWS, 128:256]))
                finish(PLANES // 2 * g + a, values)

        def body(h, carry):
            g = first + 2 * h
            if before is not None:
                before(g + 1)
            out = multiply(LHA)
            prepare(g + 1, LHB)
            complete(g, out)
            later = jnp.minimum(g + 2, last - 1)
            if before is not None:
                pl.when(g + 2 < last)(lambda: before(later))
            out = multiply(LHB)
            prepare(later, LHA)
            complete(g + 1, out)
            return carry

        if before is not None:
            before(first)
        prepare(first, LHA)
        lax.fori_loop(0, (last - first) // 2, body, 0)

    def shift_of(step, c):
        total = off[0, c]
        return total + off[1, c] if step else total

    def sizes(step):
        reach = 8 * (step + 1)
        margin = reach + 8
        ext = ROWS + 2 * margin
        return margin, ext, ext // 2, margin + reach

    def exchange_begin(k, step, sources):
        margin, ext, half, count = sizes(step)
        for a, source in enumerate(sources):
            def add(c, acc, source=source):
                start = pl.multiple_of(c * 144, 8) + 40 - margin - shift_of(step, c)
                return acc + source[pl.ds(start, ext), :]

            OWN[k, a, 0:ext] = lax.fori_loop(0, CHANS, add, jnp.zeros((ext, 128), F32))
        arrays = len(sources)
        theirs = pl.ds(pl.multiple_of((1 - core) * half, 8), half)
        return [
            send(OWN.at[k, pl.ds(0, arrays), theirs], RXA.at[k, pl.ds(0, arrays), pl.ds(0, half)],
                 tx_ss.at[k, 0], rx_rs.at[k, 0], (tm, sib))
        ]

    def exchange_middle(k, step, copies, arrays, fields):
        margin, ext, half, count = sizes(step)
        for e, field in enumerate(fields):
            ES[k, e, 0] = field[pl.ds(ROWS - 1, 64, stride=ROWS), :]
            ES[k, e, 1] = field[pl.ds(0, 64, stride=ROWS), :]
        copies[0].wait_recv()
        mine = pl.ds(pl.multiple_of(core * half, 8), half)
        for a in range(arrays):
            HS[k, a, 0:half] = OWN[k, a, mine, :] + RXA[k, a, 0:half]
        every = pl.ds(0, arrays)
        start = pl.multiple_of(core * (64 - half) + (1 - core) * 8, 8)
        rim = HS.at[k, every, pl.ds(start, count)]
        copies.append(send(rim, RXD.at[k, every, pl.ds(0, count)], tx_ss.at[k, 1], rx_rs.at[k, 1], (side_tm, far_sib)))
        copies.append(send(rim, RXM.at[k, every, pl.ds(0, count)], tx_ss.at[k, 2], rx_rs.at[k, 2], (side_tm, sib)))
        copies.append(
            send(HS.at[k, every, pl.ds(0, half)], RXF.at[k, every, pl.ds(0, half)], tx_ss.at[k, 3], rx_rs.at[k, 3],
                 (tm, far))
        )
        several = pl.ds(0, len(fields))
        copies.append(send(ES.at[k, several, 0], ER.at[k, several, 0], tx_ss.at[k, 5], rx_rs.at[k, 5], (nxt, chan)))
        copies.append(send(ES.at[k, several, 1], ER.at[k, several, 1], tx_ss.at[k, 6], rx_rs.at[k, 6], (prv, chan)))

    def exchange_end(k, step, copies, arrays):
        margin, ext, half, count = sizes(step)
        for copy in copies[1:4]:
            copy.wait_recv()
        base = pl.multiple_of(core * half, 8)
        rim = pl.multiple_of(core * half + core * (half - count), 8)
        for a in range(arrays):
            TT[k, a, pl.ds(base, half), :] = HS[k, a, 0:half] + RXF[k, a, 0:half]
            TT[k, a, pl.ds(rim, count), :] = TT[k, a, pl.ds(rim, count), :] + RXM[k, a, 0:count] + RXD[k, a, 0:count]
        block = TT.at[k, pl.ds(0, arrays), pl.ds(base, half)]
        last = send(block, block, tx_ss.at[k, 4], rx_rs.at[k, 4], (tm, sib))
        last.wait()
        copies[0].wait_send()
        for copy in copies[1:4]:
            copy.wait_send()
        for copy in copies[4:]:
            copy.wait()

    def edge_rows(k, a, source, step):
        margin = sizes(step)[0]
        for c in range(CHANS):
            start = margin + shift_of(step, c)
            TE[k, a, 0, c : c + 1] = source[pl.ds(start - 1, 1), :]
            TE[k, a, 1, c : c + 1] = source[pl.ds(start + ROWS, 1), :]

    def edge_planes(k, e, side):
        return [ER.at[k, e, side][pl.ds(q, CHANS, stride=4), :] for q in range(4)]

    def put_edge(side, planes):
        row = 7 if side == 0 else 72
        for q in range(4):
            S[pl.ds(q * 80 + row, CHANS, stride=320), :] = planes[q]

    def load_x(cp, comp, d):
        return X[cp, pl.ds(8 + 2 * d + comp, ROWS, stride=2), :]

    def load_s(cp, comp, d):
        return S[plane(2 * cp + comp, 80, 8 + d), :]

    def field(ref, c, q):
        return ref[plane(4 * c + q, ROWS, 0), :]

    def rows(ref, c):
        return ref[plane(c, ROWS, 0), :]

    def middle(ref, c):
        return ref[plane(c, 144, 40), :]

    def keep_1(c, values):
        power = jnp.zeros((ROWS, 128), F32)
        for pol in range(2):
            re, im = values[pol]
            D1[plane(4 * c + 2 * pol, ROWS, 0), :] = re
            D1[plane(4 * c + 2 * pol + 1, ROWS, 0), :] = im
            power = power + re * re + im * im
        PP[plane(c, 144, 40), :] = power
        ca, sa = sincos(NONLINEAR * power)
        CA1[plane(c, ROWS, 0), :] = ca
        SA1[plane(c, ROWS, 0), :] = sa

    def wait_load(g):
        launch_load(g).wait()

    apply_filter(load_x, TF, keep_1, 0, EARLY, wait_load)
    pl.semaphore_wait(barrier, len(peers))
    edge_copies = [
        send(launch.at[:, pl.ds(120, 8)], XE.at[0], edge_ss.at[0], edge_rs.at[0], (nxt, chan)),
        send(launch.at[:, pl.ds(0, 8)], XE.at[1], edge_ss.at[1], edge_rs.at[1], (prv, chan)),
    ]
    cot_copies = move_cot(0)
    apply_filter(load_x, TF, keep_1, EARLY, GROUPS, wait_load)
    for copy in edge_copies:
        copy.wait()
    for cp in range(32):
        EV[0, 2 * cp : 2 * cp + 2] = XE[0, cp, 6:8]
        EV[1, 2 * cp : 2 * cp + 2] = XE[1, cp, 0:2]
    short = lax.broadcasted_iota(jnp.int32, (32, 128), 1)
    pieces = []
    for side in range(2):
        inside = short >= HALF if side == 0 else short < HALF
        parts = [jnp.where(inside, EV.at[side][pl.ds(comp, 32, stride=2), :], 0.0) for comp in range(2)]
        high, low = split(jnp.concatenate(parts, axis=1))
        pieces.append(jnp.concatenate([high, low, high], axis=1))
    rim_table = jnp.concatenate([TF[256:512], TF[768:1024], TF[1280:1536]], axis=0)
    added = jnp.dot(jnp.concatenate(pieces, axis=0), rim_table, preferred_element_type=F32)
    OC[0] = added[:, 0:128]
    OC[1] = added[:, 128:256]
    for side in range(2):
        row = 0 if side == 0 else ROWS - 1
        power = jnp.zeros((CHANS, 128), F32)
        for q in range(4):
            place = pl.ds(q * ROWS + row, CHANS, stride=4 * ROWS)
            value = D1[place, :] + OC.at[q % 2][pl.ds(32 * side + q // 2, CHANS, stride=2), :]
            D1[place, :] = value
            power = power + value * value
        PP[pl.ds(40 + row, CHANS, stride=144), :] = power
        ca, sa = sincos(NONLINEAR * power)
        CA1[pl.ds(row, CHANS, stride=ROWS), :] = ca
        SA1[pl.ds(row, CHANS, stride=ROWS), :] = sa

    copies = exchange_begin(0, 0, [PP])
    exchange_middle(0, 0, copies, 1, [D1])
    cot_copies += move_cot(1)
    exchange_end(0, 0, copies, 1)

    def turn(k):
        ext = sizes(k)[1]
        ct, st = sincos(2.0 * NONLINEAR * TT[k, 0, 0:ext])
        TH[k, 0, 0:ext] = ct
        TH[k, 1, 0:ext] = st

    turn(0)
    edge_rows(0, 0, TH.at[0, 0], 0)
    edge_rows(0, 1, TH.at[0, 1], 0)

    def rotate_1(c, carry):
        start = pl.ds(16 + shift_of(0, c), ROWS)
        ct, st = TH[0, 0, start, :], TH[0, 1, start, :]
        ca, sa = rows(CA1, c), rows(SA1, c)
        cs, sn = ct * ca + st * sa, st * ca - ct * sa
        CP1[plane(c, ROWS, 0), :] = cs
        SP1[plane(c, ROWS, 0), :] = sn
        for pol in range(2):
            re, im = field(D1, c, 2 * pol), field(D1, c, 2 * pol + 1)
            S[plane(4 * c + 2 * pol, 80, 8), :] = re * cs - im * sn
            S[plane(4 * c + 2 * pol + 1, 80, 8), :] = re * sn + im * cs
        return carry

    lax.fori_loop(0, CHANS, rotate_1, 0)
    for side in range(2):
        e = edge_planes(0, 0, side)
        ca, sa = sincos(NONLINEAR * (e[0] * e[0] + e[1] * e[1] + e[2] * e[2] + e[3] * e[3]))
        ct, st = TE[0, 0, side], TE[0, 1, side]
        cs, sn = ct * ca + st * sa, st * ca - ct * sa
        put_edge(side, [e[0] * cs - e[1] * sn, e[0] * sn + e[1] * cs, e[2] * cs - e[3] * sn, e[2] * sn + e[3] * cs])

    def keep_2(c, values):
        power = jnp.zeros((ROWS, 128), F32)
        for pol in range(2):
            re, im = values[pol]
            power = power + re * re + im * im
        PP[plane(c, 144, 40), :] = power
        ca, sa = sincos(NONLINEAR * power)
        CP2[plane(c, ROWS, 0), :] = ca
        SP2[plane(c, ROWS, 0), :] = sa
        for pol in range(2):
            re, im = values[pol]
            D2[plane(4 * c + 2 * pol, ROWS, 0), :] = re
            D2[plane(4 * c + 2 * pol + 1, ROWS, 0), :] = im
            W[4 * c + 2 * pol, 16:80] = re * ca + im * sa
            W[4 * c + 2 * pol + 1, 16:80] = im * ca - re * sa

    apply_filter(load_s, TF, keep_2)
    cot_copy.wait()
    for copy in cot_copies:
        copy.wait()

    def project_2(c, carry):
        shift = shift_of(1, c)
        ca, sa = rows(CP2, c), rows(SP2, c)
        zr, zi = jnp.zeros((ROWS, 128), F32), jnp.zeros((ROWS, 128), F32)
        for pol in range(2):
            re, im = field(D2, c, 2 * pol), field(D2, c, 2 * pol + 1)
            gr = C[2 * c + pol, pl.ds(32 + 2 * shift, ROWS, stride=2), :]
            gi = C[2 * c + pol, pl.ds(33 + 2 * shift, ROWS, stride=2), :]
            hr = gr * ca - gi * sa
            hi = gr * sa + gi * ca
            R[plane(4 * c + 2 * pol, ROWS, 0), :] = hr
            R[plane(4 * c + 2 * pol + 1, ROWS, 0), :] = hi
            zr = zr + hr * re + hi * im
            zi = zi + hi * re - hr * im
        ZR[plane(c, 144, 40), :] = zr
        ZI[plane(c, 144, 40), :] = zi
        return carry

    lax.fori_loop(0, CHANS, project_2, 0)
    copies = exchange_begin(1, 1, [PP, ZR, ZI])
    exchange_middle(1, 1, copies, 3, [D2, R])
    def move_arrival(part, start, size):
        planes = pl.ds(start, size)
        return [
            send(W.at[planes, pl.ds(64, 16)], W.at[planes, pl.ds(0, 16)], w_ss.at[part, 0], w_rs.at[part, 0],
                 (nxt, chan)),
            send(W.at[planes, pl.ds(16, 16)], W.at[planes, pl.ds(80, 16)], w_ss.at[part, 1], w_rs.at[part, 1],
                 (prv, chan)),
        ]

    w_copies = move_arrival(0, 0, 16)
    exchange_end(1, 1, copies, 3)
    w_copies += move_arrival(2, 16, 32)
    turn(1)
    TT[1, 0] = TT[1, 2] * TH[1, 0] - TT[1, 1] * TH[1, 1]
    edge_rows(1, 0, TH.at[1, 0], 1)
    edge_rows(1, 1, TH.at[1, 1], 1)
    edge_rows(1, 2, TT.at[1, 0], 1)

    def weigh_2(c, carry):
        start = pl.ds(24 + shift_of(1, c), ROWS)
        ct, st, total = TH[1, 0, start, :], TH[1, 1, start, :], TT[1, 0, start, :]
        own = middle(ZI, c) * ct - middle(ZR, c) * st
        w = 2.0 * NONLINEAR * (2.0 * total - own)
        for pol in range(2):
            rr, ri = field(R, c, 2 * pol), field(R, c, 2 * pol + 1)
            S[plane(4 * c + 2 * pol, 80, 8), :] = rr * ct + ri * st + w * field(D2, c, 2 * pol)
            S[plane(4 * c + 2 * pol + 1, 80, 8), :] = ri * ct - rr * st + w * field(D2, c, 2 * pol + 1)
        return carry

    lax.fori_loop(0, CHANS, weigh_2, 0)
    for side in range(2):
        d, r = edge_planes(1, 0, side), edge_planes(1, 1, side)
        ct, st = TE[1, 0, side], TE[1, 1, side]
        rr = [r[0] * ct + r[1] * st, r[1] * ct - r[0] * st, r[2] * ct + r[3] * st, r[3] * ct - r[2] * st]
        own = rr[1] * d[0] - rr[0] * d[1] + rr[3] * d[2] - rr[2] * d[3]
        w = 2.0 * NONLINEAR * (2.0 * TE[1, 2, side] - own)
        put_edge(side, [rr[q] + w * d[q] for q in range(4)])

    def back_rotate(c, values):
        cs, sn = rows(CP1, c), rows(SP1, c)
        own = jnp.zeros((ROWS, 128), F32)
        for pol in range(2):
            re, im = values[pol]
            rr = re * cs + im * sn
            ri = im * cs - re * sn
            R[plane(4 * c + 2 * pol, ROWS, 0), :] = rr
            R[plane(4 * c + 2 * pol + 1, ROWS, 0), :] = ri
            own = own + ri * field(D1, c, 2 * pol) - rr * field(D1, c, 2 * pol + 1)
        PP[plane(c, 144, 40), :] = own

    apply_filter(load_s, TB, back_rotate)
    copies = exchange_begin(2, 0, [PP])
    exchange_middle(2, 0, copies, 1, [R])
    w_copies += move_arrival(1, 48, 16)
    exchange_end(2, 0, copies, 1)
    edge_rows(2, 0, TT.at[2, 0], 0)

    def weigh_1(c, carry):
        total = TT[2, 0, pl.ds(16 + shift_of(0, c), ROWS), :]
        w = 2.0 * NONLINEAR * (2.0 * total - middle(PP, c))
        for q in range(4):
            S[plane(4 * c + q, 80, 8), :] = field(R, c, q) + w * field(D1, c, q)
        return carry

    lax.fori_loop(0, CHANS, weigh_1, 0)
    for side in range(2):
        r, d = edge_planes(2, 0, side), edge_planes(0, 0, side)
        own = r[1] * d[0] - r[0] * d[1] + r[3] * d[2] - r[2] * d[3]
        w = 2.0 * NONLINEAR * (2.0 * TE[2, 0, side] - own)
        put_edge(side, [r[q] + w * d[q] for q in range(4)])

    for copy in w_copies:
        copy.wait()

    def put_results(c, values):
        start = pl.ds(16 - shift_of(1, c), ROWS)
        ct, st = TH[1, 0, 24:88], TH[1, 1, 24:88]
        for pol in range(2):
            for comp in range(2):
                grad[2 * c + pol, pl.ds(comp, ROWS, stride=2), :] = values[pol][comp]
            re, im = W[4 * c + 2 * pol, start, :], W[4 * c + 2 * pol + 1, start, :]
            arr[2 * c + pol, pl.ds(0, ROWS, stride=2), :] = re * ct - im * st
            arr[2 * c + pol, pl.ds(1, ROWS, stride=2), :] = re * st + im * ct

    apply_filter(load_s, TB, put_results)


def rows_of(x):
    return x.reshape(32, 2, ROWS, 128).transpose(0, 2, 1, 3).reshape(32, 2 * ROWS, 128)


def field_of(x):
    return x.reshape(32, ROWS, 2, 128).transpose(0, 2, 1, 3).reshape(16, 2, 2, ROWS * 128)


def solution(mesh):
    n = mesh.shape["tm"]

    def local(launch, cotangent, filter_taps, offsets):
        out = jax.ShapeDtypeStruct((32, 2 * ROWS, 128), F32)
        anywhere = pl.BlockSpec(memory_space=pl.ANY)
        dma = pltpu.SemaphoreType.DMA
        arrival, gradient = pl.pallas_call(
            functools.partial(kernel, n),
            out_shape=(pltpu.VMEM((32, 2 * ROWS, 128), F32), pltpu.VMEM((32, 2 * ROWS, 128), F32)),
            in_specs=[
                anywhere,
                anywhere,
                pl.BlockSpec(memory_space=pltpu.VMEM),
                pl.BlockSpec(memory_space=pltpu.SMEM),
            ],
            out_specs=(pl.BlockSpec(memory_space=pltpu.VMEM), pl.BlockSpec(memory_space=pltpu.VMEM)),
            scratch_shapes=[
                pltpu.VMEM((32, 144, 128), F32),
                pltpu.VMEM((64 * 80, 128), F32),
                pltpu.VMEM((64 * ROWS, 128), F32),
                pltpu.VMEM((64 * ROWS, 128), F32),
                pltpu.VMEM((CHANS * ROWS, 128), F32),
                pltpu.VMEM((CHANS * ROWS, 128), F32),
                pltpu.VMEM((CHANS * ROWS, 128), F32),
                pltpu.VMEM((CHANS * ROWS, 128), F32),
                pltpu.VMEM((CHANS * ROWS, 128), F32),
                pltpu.VMEM((CHANS * ROWS, 128), F32),
                pltpu.VMEM((32, 192, 128), F32),
                pltpu.VMEM((64 * ROWS, 128), F32),
                pltpu.VMEM((64, 96, 128), F32),
                pltpu.VMEM((PLANES * ROWS, 1024), BF16),
                pltpu.VMEM((PLANES * ROWS, 1024), BF16),
                pltpu.VMEM((CHANS * 144, 128), F32),
                pltpu.VMEM((CHANS * 144, 128), F32),
                pltpu.VMEM((CHANS * 144, 128), F32),
                pltpu.VMEM((2, 2, 112, 128), F32),
                pltpu.VMEM((3, 3, 2, CHANS, 128), F32),
                pltpu.VMEM((3, 3, 112, 128), F32),
                pltpu.VMEM((3, 3, 56, 128), F32),
                pltpu.VMEM((3, 3, 56, 128), F32),
                pltpu.VMEM((3, 3, 40, 128), F32),
                pltpu.VMEM((3, 3, 40, 128), F32),
                pltpu.VMEM((3, 3, 56, 128), F32),
                pltpu.VMEM((3, 3, 112, 128), F32),
                pltpu.VMEM((3, 2, 2, 64, 128), F32),
                pltpu.VMEM((3, 2, 2, 64, 128), F32),
                pltpu.VMEM((2, 32, 8, 128), F32),
                pltpu.VMEM((2, 64, 128), F32),
                pltpu.VMEM((2, 64, 128), F32),
                pltpu.VMEM((1536, 256), BF16),
                pltpu.VMEM((1536, 256), BF16),
                dma((GROUPS,)),
                dma((2,)),
                dma((2,)),
                dma((1,)),
                dma((2, 2)),
                dma((2, 2)),
                dma((3, 7)),
                dma((3, 7)),
                dma((4, 2)),
                dma((4, 2)),
            ],
            compiler_params=pltpu.CompilerParams(
                collective_id=0, has_side_effects=True, vmem_limit_bytes=56 * 1024 * 1024
            ),
        )(rows_of(launch), rows_of(cotangent), filter_taps, offsets)
        return field_of(arrival), field_of(gradient)

    placed = (P("chan", None, None, "tm"), P("chan", None, None, "tm"), P(), P(None, "chan"))
    return jax.shard_map(
        local,
        mesh=mesh,
        in_specs=placed,
        out_specs=(P("chan", None, None, "tm"), P("chan", None, None, "tm")),
        check_vma=False,
    )
```

```python
import functools

import jax
import jax.numpy as jnp
from jax import lax
from jax.experimental import pallas as pl
from jax.experimental.pallas import tpu as pltpu
from jax.sharding import PartitionSpec as P

NONLINEAR = 0.001953125
ROWS = 64
HALF = 64
GROUPS = 4
EARLY = 2
PLANES = 32 // GROUPS
CHANS = 16
MESH = pl.DeviceIdType.MESH
F32 = jnp.float32
BF16 = jnp.bfloat16


def sincos(x):
    k = jnp.floor(x * 0.6366197723675814 + 0.5)
    r = x - k * 1.5703125
    r = r - k * 4.837512969970703125e-4
    r = r - k * 7.549789948768648e-8
    n = k.astype(jnp.int32)
    r2 = r * r
    s = r + r * r2 * (-1.6666654611e-1 + r2 * (8.3321608736e-3 - r2 * 1.9515295891e-4))
    c = 1.0 - 0.5 * r2 + r2 * r2 * (4.166664568298827e-2 + r2 * (2.443315711809948e-5 * r2 - 1.388731625493765e-3))
    swap = (n & 1) == 1
    sine = jnp.where(swap, c, s)
    cosine = jnp.where(swap, s, c)
    sine = jnp.where((n & 2) == 2, -sine, sine)
    cosine = jnp.where(((n + 1) & 2) == 2, -cosine, cosine)
    return cosine, sine


def split(x):
    high = x.astype(BF16)
    low = (x - high.astype(F32)).astype(BF16)
    return high, low


def plane(index, pitch, first):
    return pl.ds(pl.multiple_of(index * pitch, 8) + first, ROWS)


def build_tables(taps, forward, backward):
    row = lax.broadcasted_iota(jnp.int32, (128, 128), 0)
    col = lax.broadcasted_iota(jnp.int32, (128, 128), 1)
    lag = col - row
    mats = []
    for comp in range(2):
        body = jnp.broadcast_to(taps[comp : comp + 1, 0:128], (128, 128))
        last = jnp.broadcast_to(taps[comp : comp + 1, 128:129], (128, 128))
        minus = pltpu.roll(body, HALF, 1)
        plus = jnp.where(col == HALF, last, minus)
        minus = pltpu.roll(minus, 0, 1, stride=1, stride_axis=0)
        plus = pltpu.roll(plus, 0, 1, stride=1, stride_axis=0)
        centre = jnp.where(lag == -HALF, minus, plus)
        centre = jnp.where((lag >= -HALF) & (lag <= HALF), centre, 0.0)
        rim = jnp.where(lag == HALF, minus, plus)
        rim = jnp.where((lag <= -HALF) | (lag >= HALF), rim, 0.0)
        mats.append((centre, rim))
    for table, adjoint in ((forward, False), (backward, True)):
        for part in range(2):
            real, imag = mats[0][part], mats[1][part]
            if adjoint:
                real, imag = real.T, -imag.T
            for place, block in ((0, (real, imag)), (1, (-imag, real))):
                start = part * 256 + place * 128
                for side in range(2):
                    high, low = split(block[side])
                    cols = slice(side * 128, side * 128 + 128)
                    table[start : start + 128, cols] = high
                    table[512 + start : 512 + start + 128, cols] = high
                    table[1024 + start : 1024 + start + 128, cols] = low


def kernel(n, launch, cot, taps, off, arr, grad, X, S, D1, D2, CA1, SA1, CP1, SP1, CP2, SP2, C, R, W, LHA, LHB, PP, ZR, ZI, TH, TE,
           OWN, RXA, RXF, RXM, RXD, HS, TT, ES, ER, XE, EV, OC, TF, TB, load_sem, edge_ss, edge_rs,
           cot_sem, cot_ss, cot_rs, tx_ss, rx_rs, w_ss, w_rs):
    tm, chan = lax.axis_index("tm"), lax.axis_index("chan")
    nxt, prv = lax.rem(tm + 1, n), lax.rem(tm + n - 1, n)
    core = lax.rem(chan, 2)
    sib = chan + 1 - 2 * core
    far = lax.rem(chan + 2, 4)
    far_sib = lax.rem(sib + 2, 4)
    side_tm = core * nxt + (1 - core) * prv

    def launch_load(g):
        return pltpu.make_async_copy(
            launch.at[pl.ds(PLANES * g, PLANES)], X.at[pl.ds(PLANES * g, PLANES), pl.ds(8, 128)], load_sem.at[g]
        )

    for g in range(GROUPS):
        launch_load(g).start()
    barrier = pltpu.get_barrier_semaphore()
    peers = [(tm, sib), (tm, far), (nxt, chan), (prv, chan), (side_tm, sib), (side_tm, far_sib)]
    for peer in peers:
        pl.semaphore_signal(barrier, inc=1, device_id=peer, device_id_type=MESH)
    cot_copy = pltpu.make_async_copy(cot, C.at[:, pl.ds(32, 128)], cot_sem.at[0])
    cot_copy.start()

    def send(src, dst, ss, rs, peer):
        copy = pltpu.make_async_remote_copy(
            src_ref=src, dst_ref=dst, send_sem=ss, recv_sem=rs, device_id=peer, device_id_type=MESH
        )
        copy.start()
        return copy

    def move_cot(half):
        cps = pl.ds(16 * half, 16)
        return [
            send(cot.at[cps, pl.ds(96, 32)], C.at[cps, pl.ds(0, 32)], cot_ss.at[half, 0], cot_rs.at[half, 0],
                 (nxt, chan)),
            send(cot.at[cps, pl.ds(0, 32)], C.at[cps, pl.ds(160, 32)], cot_ss.at[half, 1], cot_rs.at[half, 1],
                 (prv, chan)),
        ]

    build_tables(taps, TF, TB)
    for buffer in (PP, ZR, ZI):
        for c in range(CHANS):
            buffer[c * 144 : c * 144 + 40] = jnp.zeros((40, 128), F32)
            buffer[c * 144 + 104 : c * 144 + 144] = jnp.zeros((40, 128), F32)
    X[:, 0:8] = jnp.zeros((32, 8, 128), F32)
    X[:, 136:144] = jnp.zeros((32, 8, 128), F32)
    lane = lax.broadcasted_iota(jnp.int32, (ROWS, 128), 1)
    short = lax.broadcasted_iota(jnp.int32, (32, 128), 1)

    def apply_filter(load, table, finish, first=0, last=GROUPS, before=None):
        def prepare(g, LH):
            for j in range(PLANES):
                for comp in range(2):
                    x = load(PLANES * g + j, comp, 0)
                    z = jnp.where(lane < HALF, load(PLANES * g + j, comp, 1), load(PLANES * g + j, comp, -1))
                    for place, value in ((comp, x), (2 + comp, z)):
                        high, low = split(value)
                        LH[j * ROWS : j * ROWS + ROWS, place * 128 : place * 128 + 128] = high
                        LH[j * ROWS : j * ROWS + ROWS, 512 + place * 128 : 640 + place * 128] = low

        def multiply(LH):
            out = jnp.dot(LH[...], table[0:1024], preferred_element_type=F32)
            return out + jnp.dot(LH[:, 0:512], table[1024:1536], preferred_element_type=F32)

        def complete(g, out):
            for a in range(PLANES // 2):
                values = []
                for pol in range(2):
                    start = (2 * a + pol) * ROWS
                    values.append((out[start : start + ROWS, 0:128], out[start : start + ROWS, 128:256]))
                finish(PLANES // 2 * g + a, values)

        def body(h, carry):
            g = first + 2 * h
            if before is not None:
                before(g + 1)
            out = multiply(LHA)
            prepare(g + 1, LHB)
            complete(g, out)
            later = jnp.minimum(g + 2, last - 1)
            if before is not None:
                pl.when(g + 2 < last)(lambda: before(later))
            out = multiply(LHB)
            prepare(later, LHA)
            complete(g + 1, out)
            return carry

        if before is not None:
            before(first)
        prepare(first, LHA)
        lax.fori_loop(0, (last - first) // 2, body, 0)

    def shift_of(step, c):
        total = off[0, c]
        return total + off[1, c] if step else total

    def sizes(step):
        reach = 8 * (step + 1)
        margin = reach + 8
        ext = ROWS + 2 * margin
        return margin, ext, ext // 2, margin + reach

    def exchange_begin(k, step, sources):
        margin, ext, half, count = sizes(step)
        for a, source in enumerate(sources):
            def add(c, acc, source=source):
                start = pl.multiple_of(c * 144, 8) + 40 - margin - shift_of(step, c)
                return acc + source[pl.ds(start, ext), :]

            OWN[k, a, 0:ext] = lax.fori_loop(0, CHANS, add, jnp.zeros((ext, 128), F32), unroll=4)
        arrays = len(sources)
        theirs = pl.ds(pl.multiple_of((1 - core) * half, 8), half)
        return [
            send(OWN.at[k, pl.ds(0, arrays), theirs], RXA.at[k, pl.ds(0, arrays), pl.ds(0, half)],
                 tx_ss.at[k, 0], rx_rs.at[k, 0], (tm, sib))
        ]

    def exchange_middle(k, step, copies, arrays, fields):
        margin, ext, half, count = sizes(step)
        for e, field in enumerate(fields):
            for side, row in ((0, ROWS - 1), (1, 0)):
                one = field[pl.ds(row, 32, stride=2 * ROWS), :]
                two = field[pl.ds(ROWS + row, 32, stride=2 * ROWS), :]
                if side == 0:
                    one = pltpu.roll(one, HALF, 1)
                else:
                    two = pltpu.roll(two, HALF, 1)
                ES[k, e, side] = jnp.where(short < HALF, one, two)
        copies[0].wait_recv()
        mine = pl.ds(pl.multiple_of(core * half, 8), half)
        for a in range(arrays):
            HS[k, a, 0:half] = OWN[k, a, mine, :] + RXA[k, a, 0:half]
        every = pl.ds(0, arrays)
        start = pl.multiple_of(core * (64 - half) + (1 - core) * 8, 8)
        rim = HS.at[k, every, pl.ds(start, count)]
        copies.append(send(rim, RXD.at[k, every, pl.ds(0, count)], tx_ss.at[k, 1], rx_rs.at[k, 1], (side_tm, far_sib)))
        copies.append(send(rim, RXM.at[k, every, pl.ds(0, count)], tx_ss.at[k, 2], rx_rs.at[k, 2], (side_tm, sib)))
        copies.append(
            send(HS.at[k, every, pl.ds(0, half)], RXF.at[k, every, pl.ds(0, half)], tx_ss.at[k, 3], rx_rs.at[k, 3],
                 (tm, far))
        )
        several = pl.ds(0, len(fields))
        copies.append(send(ES.at[k, several, 0], ER.at[k, several, 0], tx_ss.at[k, 5], rx_rs.at[k, 5], (nxt, chan)))
        copies.append(send(ES.at[k, several, 1], ER.at[k, several, 1], tx_ss.at[k, 6], rx_rs.at[k, 6], (prv, chan)))

    def exchange_end(k, step, copies, arrays):
        margin, ext, half, count = sizes(step)
        for copy in copies[1:4]:
            copy.wait_recv()
        base = pl.multiple_of(core * half, 8)
        rim = pl.multiple_of(core * half + core * (half - count), 8)
        for a in range(arrays):
            TT[k, a, pl.ds(base, half), :] = HS[k, a, 0:half] + RXF[k, a, 0:half]
            TT[k, a, pl.ds(rim, count), :] = TT[k, a, pl.ds(rim, count), :] + RXM[k, a, 0:count] + RXD[k, a, 0:count]
        block = TT.at[k, pl.ds(0, arrays), pl.ds(base, half)]
        last = send(block, block, tx_ss.at[k, 4], rx_rs.at[k, 4], (tm, sib))
        last.wait()
        copies[0].wait_send()
        for copy in copies[1:4]:
            copy.wait_send()
        for copy in copies[4:]:
            copy.wait()

    def edge_rows(k, a, source, step):
        margin = sizes(step)[0]
        for c in range(CHANS):
            start = margin + shift_of(step, c)
            TE[k, a, 0, c : c + 1] = source[pl.ds(start - 1, 1), :]
            TE[k, a, 1, c : c + 1] = source[pl.ds(start + ROWS, 1), :]

    def edge_planes(k, e, side):
        planes = []
        for q in range(4):
            both = ER.at[k, e, side][pl.ds(q // 2, CHANS, stride=2), :]
            planes.append(pltpu.roll(both, HALF, 1) if q % 2 == side else both)
        return planes

    def put_edge(side, planes):
        row = 7 if side == 0 else 72
        for q in range(4):
            S[pl.ds(q * 80 + row, CHANS, stride=320), :] = planes[q]

    def load_x(cp, comp, d):
        return X[cp, pl.ds(8 + 2 * d + comp, ROWS, stride=2), :]

    def load_s(cp, comp, d):
        return S[plane(2 * cp + comp, 80, 8 + d), :]

    def field(ref, c, q):
        return ref[plane(4 * c + q, ROWS, 0), :]

    def rows(ref, c):
        return ref[plane(c, ROWS, 0), :]

    def middle(ref, c):
        return ref[plane(c, 144, 40), :]

    def keep_1(c, values):
        power = jnp.zeros((ROWS, 128), F32)
        for pol in range(2):
            re, im = values[pol]
            D1[plane(4 * c + 2 * pol, ROWS, 0), :] = re
            D1[plane(4 * c + 2 * pol + 1, ROWS, 0), :] = im
            power = power + re * re + im * im
        PP[plane(c, 144, 40), :] = power
        ca, sa = sincos(NONLINEAR * power)
        CA1[plane(c, ROWS, 0), :] = ca
        SA1[plane(c, ROWS, 0), :] = sa

    def wait_load(g):
        launch_load(g).wait()

    apply_filter(load_x, TF, keep_1, 0, EARLY, wait_load)
    pl.semaphore_wait(barrier, len(peers))
    edge_copies = [
        send(launch.at[:, pl.ds(120, 8)], XE.at[0], edge_ss.at[0], edge_rs.at[0], (nxt, chan)),
        send(launch.at[:, pl.ds(0, 8)], XE.at[1], edge_ss.at[1], edge_rs.at[1], (prv, chan)),
    ]
    cot_copies = move_cot(0)
    apply_filter(load_x, TF, keep_1, EARLY, GROUPS, wait_load)
    for copy in edge_copies:
        copy.wait()
    for cp in range(32):
        EV[0, 2 * cp : 2 * cp + 2] = XE[0, cp, 6:8]
        EV[1, 2 * cp : 2 * cp + 2] = XE[1, cp, 0:2]
    pieces = []
    for side in range(2):
        inside = short >= HALF if side == 0 else short < HALF
        parts = [jnp.where(inside, EV.at[side][pl.ds(comp, 32, stride=2), :], 0.0) for comp in range(2)]
        high, low = split(jnp.concatenate(parts, axis=1))
        pieces.append(jnp.concatenate([high, low, high], axis=1))
    rim_table = jnp.concatenate([TF[256:512], TF[768:1024], TF[1280:1536]], axis=0)
    added = jnp.dot(jnp.concatenate(pieces, axis=0), rim_table, preferred_element_type=F32)
    OC[0] = added[:, 0:128]
    OC[1] = added[:, 128:256]
    for side in range(2):
        row = 0 if side == 0 else ROWS - 1
        power = jnp.zeros((CHANS, 128), F32)
        for q in range(4):
            place = pl.ds(q * ROWS + row, CHANS, stride=4 * ROWS)
            value = D1[place, :] + OC.at[q % 2][pl.ds(32 * side + q // 2, CHANS, stride=2), :]
            D1[place, :] = value
            power = power + value * value
        PP[pl.ds(40 + row, CHANS, stride=144), :] = power
        ca, sa = sincos(NONLINEAR * power)
        CA1[pl.ds(row, CHANS, stride=ROWS), :] = ca
        SA1[pl.ds(row, CHANS, stride=ROWS), :] = sa

    copies = exchange_begin(0, 0, [PP])
    exchange_middle(0, 0, copies, 1, [D1])
    cot_copies += move_cot(1)
    exchange_end(0, 0, copies, 1)

    def turn(k):
        ext = sizes(k)[1]
        ct, st = sincos(2.0 * NONLINEAR * TT[k, 0, 0:ext])
        TH[k, 0, 0:ext] = ct
        TH[k, 1, 0:ext] = st

    turn(0)
    edge_rows(0, 0, TH.at[0, 0], 0)
    edge_rows(0, 1, TH.at[0, 1], 0)

    def rotate_1(c, carry):
        start = pl.ds(16 + shift_of(0, c), ROWS)
        ct, st = TH[0, 0, start, :], TH[0, 1, start, :]
        ca, sa = rows(CA1, c), rows(SA1, c)
        cs, sn = ct * ca + st * sa, st * ca - ct * sa
        CP1[plane(c, ROWS, 0), :] = cs
        SP1[plane(c, ROWS, 0), :] = sn
        for pol in range(2):
            re, im = field(D1, c, 2 * pol), field(D1, c, 2 * pol + 1)
            S[plane(4 * c + 2 * pol, 80, 8), :] = re * cs - im * sn
            S[plane(4 * c + 2 * pol + 1, 80, 8), :] = re * sn + im * cs
        return carry

    lax.fori_loop(0, CHANS, rotate_1, 0)
    for side in range(2):
        e = edge_planes(0, 0, side)
        ca, sa = sincos(NONLINEAR * (e[0] * e[0] + e[1] * e[1] + e[2] * e[2] + e[3] * e[3]))
        ct, st = TE[0, 0, side], TE[0, 1, side]
        cs, sn = ct * ca + st * sa, st * ca - ct * sa
        put_edge(side, [e[0] * cs - e[1] * sn, e[0] * sn + e[1] * cs, e[2] * cs - e[3] * sn, e[2] * sn + e[3] * cs])

    def keep_2(c, values):
        power = jnp.zeros((ROWS, 128), F32)
        for pol in range(2):
            re, im = values[pol]
            power = power + re * re + im * im
        PP[plane(c, 144, 40), :] = power
        ca, sa = sincos(NONLINEAR * power)
        CP2[plane(c, ROWS, 0), :] = ca
        SP2[plane(c, ROWS, 0), :] = sa
        for pol in range(2):
            re, im = values[pol]
            D2[plane(4 * c + 2 * pol, ROWS, 0), :] = re
            D2[plane(4 * c + 2 * pol + 1, ROWS, 0), :] = im
            W[4 * c + 2 * pol, 16:80] = re * ca + im * sa
            W[4 * c + 2 * pol + 1, 16:80] = im * ca - re * sa

    apply_filter(load_s, TF, keep_2)
    cot_copy.wait()
    for copy in cot_copies:
        copy.wait()

    def project_2(c, carry):
        shift = shift_of(1, c)
        ca, sa = rows(CP2, c), rows(SP2, c)
        zr, zi = jnp.zeros((ROWS, 128), F32), jnp.zeros((ROWS, 128), F32)
        for pol in range(2):
            re, im = field(D2, c, 2 * pol), field(D2, c, 2 * pol + 1)
            gr = C[2 * c + pol, pl.ds(32 + 2 * shift, ROWS, stride=2), :]
            gi = C[2 * c + pol, pl.ds(33 + 2 * shift, ROWS, stride=2), :]
            hr = gr * ca - gi * sa
            hi = gr * sa + gi * ca
            R[plane(4 * c + 2 * pol, ROWS, 0), :] = hr
            R[plane(4 * c + 2 * pol + 1, ROWS, 0), :] = hi
            zr = zr + hr * re + hi * im
            zi = zi + hi * re - hr * im
        ZR[plane(c, 144, 40), :] = zr
        ZI[plane(c, 144, 40), :] = zi
        return carry

    lax.fori_loop(0, CHANS, project_2, 0)
    copies = exchange_begin(1, 1, [PP, ZR, ZI])
    exchange_middle(1, 1, copies, 3, [D2, R])
    def move_arrival(part, start, size):
        planes = pl.ds(start, size)
        return [
            send(W.at[planes, pl.ds(64, 16)], W.at[planes, pl.ds(0, 16)], w_ss.at[part, 0], w_rs.at[part, 0],
                 (nxt, chan)),
            send(W.at[planes, pl.ds(16, 16)], W.at[planes, pl.ds(80, 16)], w_ss.at[part, 1], w_rs.at[part, 1],
                 (prv, chan)),
        ]

    w_copies = move_arrival(0, 0, 16)
    exchange_end(1, 1, copies, 3)
    w_copies += move_arrival(2, 16, 32)
    turn(1)
    TT[1, 0] = TT[1, 2] * TH[1, 0] - TT[1, 1] * TH[1, 1]
    edge_rows(1, 0, TH.at[1, 0], 1)
    edge_rows(1, 1, TH.at[1, 1], 1)
    edge_rows(1, 2, TT.at[1, 0], 1)

    def weigh_2(c, carry):
        start = pl.ds(24 + shift_of(1, c), ROWS)
        ct, st, total = TH[1, 0, start, :], TH[1, 1, start, :], TT[1, 0, start, :]
        own = middle(ZI, c) * ct - middle(ZR, c) * st
        w = 2.0 * NONLINEAR * (2.0 * total - own)
        for pol in range(2):
            rr, ri = field(R, c, 2 * pol), field(R, c, 2 * pol + 1)
            S[plane(4 * c + 2 * pol, 80, 8), :] = rr * ct + ri * st + w * field(D2, c, 2 * pol)
            S[plane(4 * c + 2 * pol + 1, 80, 8), :] = ri * ct - rr * st + w * field(D2, c, 2 * pol + 1)
        return carry

    lax.fori_loop(0, CHANS, weigh_2, 0)
    for side in range(2):
        d, r = edge_planes(1, 0, side), edge_planes(1, 1, side)
        ct, st = TE[1, 0, side], TE[1, 1, side]
        rr = [r[0] * ct + r[1] * st, r[1] * ct - r[0] * st, r[2] * ct + r[3] * st, r[3] * ct - r[2] * st]
        own = rr[1] * d[0] - rr[0] * d[1] + rr[3] * d[2] - rr[2] * d[3]
        w = 2.0 * NONLINEAR * (2.0 * TE[1, 2, side] - own)
        put_edge(side, [rr[q] + w * d[q] for q in range(4)])

    def back_rotate(c, values):
        cs, sn = rows(CP1, c), rows(SP1, c)
        own = jnp.zeros((ROWS, 128), F32)
        for pol in range(2):
            re, im = values[pol]
            rr = re * cs + im * sn
            ri = im * cs - re * sn
            R[plane(4 * c + 2 * pol, ROWS, 0), :] = rr
            R[plane(4 * c + 2 * pol + 1, ROWS, 0), :] = ri
            own = own + ri * field(D1, c, 2 * pol) - rr * field(D1, c, 2 * pol + 1)
        PP[plane(c, 144, 40), :] = own

    apply_filter(load_s, TB, back_rotate)
    copies = exchange_begin(2, 0, [PP])
    exchange_middle(2, 0, copies, 1, [R])
    w_copies += move_arrival(1, 48, 16)
    exchange_end(2, 0, copies, 1)
    edge_rows(2, 0, TT.at[2, 0], 0)

    def weigh_1(c, carry):
        total = TT[2, 0, pl.ds(16 + shift_of(0, c), ROWS), :]
        w = 2.0 * NONLINEAR * (2.0 * total - middle(PP, c))
        for q in range(4):
            S[plane(4 * c + q, 80, 8), :] = field(R, c, q) + w * field(D1, c, q)
        return carry

    lax.fori_loop(0, CHANS, weigh_1, 0)
    for side in range(2):
        r, d = edge_planes(2, 0, side), edge_planes(0, 0, side)
        own = r[1] * d[0] - r[0] * d[1] + r[3] * d[2] - r[2] * d[3]
        w = 2.0 * NONLINEAR * (2.0 * TE[2, 0, side] - own)
        put_edge(side, [r[q] + w * d[q] for q in range(4)])

    def put_results(c, values):
        for pol in range(2):
            for comp in range(2):
                grad[2 * c + pol, pl.ds(comp, ROWS, stride=2), :] = values[pol][comp]

    apply_filter(load_s, TB, put_results)
    for copy in w_copies:
        copy.wait()

    def put_arrival(c, carry):
        start = pl.ds(16 - shift_of(1, c), ROWS)
        ct, st = TH[1, 0, 24:88], TH[1, 1, 24:88]
        for pol in range(2):
            re, im = W[4 * c + 2 * pol, start, :], W[4 * c + 2 * pol + 1, start, :]
            arr[2 * c + pol, pl.ds(0, ROWS, stride=2), :] = re * ct - im * st
            arr[2 * c + pol, pl.ds(1, ROWS, stride=2), :] = re * st + im * ct
        return carry

    lax.fori_loop(0, CHANS, put_arrival, 0, unroll=2)


def rows_of(x):
    return x.reshape(32, 2, ROWS, 128).transpose(0, 2, 1, 3).reshape(32, 2 * ROWS, 128)


def field_of(x):
    return x.reshape(32, ROWS, 2, 128).transpose(0, 2, 1, 3).reshape(16, 2, 2, ROWS * 128)


def solution(mesh):
    n = mesh.shape["tm"]

    def local(launch, cotangent, filter_taps, offsets):
        out = jax.ShapeDtypeStruct((32, 2 * ROWS, 128), F32)
        anywhere = pl.BlockSpec(memory_space=pl.ANY)
        dma = pltpu.SemaphoreType.DMA
        arrival, gradient = pl.pallas_call(
            functools.partial(kernel, n),
            out_shape=(pltpu.VMEM((32, 2 * ROWS, 128), F32), pltpu.VMEM((32, 2 * ROWS, 128), F32)),
            in_specs=[
                anywhere,
                anywhere,
                pl.BlockSpec(memory_space=pltpu.VMEM),
                pl.BlockSpec(memory_space=pltpu.SMEM),
            ],
            out_specs=(pl.BlockSpec(memory_space=pltpu.VMEM), pl.BlockSpec(memory_space=pltpu.VMEM)),
            scratch_shapes=[
                pltpu.VMEM((32, 144, 128), F32),
                pltpu.VMEM((64 * 80, 128), F32),
                pltpu.VMEM((64 * ROWS, 128), F32),
                pltpu.VMEM((64 * ROWS, 128), F32),
                pltpu.VMEM((CHANS * ROWS, 128), F32),
                pltpu.VMEM((CHANS * ROWS, 128), F32),
                pltpu.VMEM((CHANS * ROWS, 128), F32),
                pltpu.VMEM((CHANS * ROWS, 128), F32),
                pltpu.VMEM((CHANS * ROWS, 128), F32),
                pltpu.VMEM((CHANS * ROWS, 128), F32),
                pltpu.VMEM((32, 192, 128), F32),
                pltpu.VMEM((64 * ROWS, 128), F32),
                pltpu.VMEM((64, 96, 128), F32),
                pltpu.VMEM((PLANES * ROWS, 1024), BF16),
                pltpu.VMEM((PLANES * ROWS, 1024), BF16),
                pltpu.VMEM((CHANS * 144, 128), F32),
                pltpu.VMEM((CHANS * 144, 128), F32),
                pltpu.VMEM((CHANS * 144, 128), F32),
                pltpu.VMEM((2, 2, 112, 128), F32),
                pltpu.VMEM((3, 3, 2, CHANS, 128), F32),
                pltpu.VMEM((3, 3, 112, 128), F32),
                pltpu.VMEM((3, 3, 56, 128), F32),
                pltpu.VMEM((3, 3, 56, 128), F32),
                pltpu.VMEM((3, 3, 40, 128), F32),
                pltpu.VMEM((3, 3, 40, 128), F32),
                pltpu.VMEM((3, 3, 56, 128), F32),
                pltpu.VMEM((3, 3, 112, 128), F32),
                pltpu.VMEM((3, 2, 2, 32, 128), F32),
                pltpu.VMEM((3, 2, 2, 32, 128), F32),
                pltpu.VMEM((2, 32, 8, 128), F32),
                pltpu.VMEM((2, 64, 128), F32),
                pltpu.VMEM((2, 64, 128), F32),
                pltpu.VMEM((1536, 256), BF16),
                pltpu.VMEM((1536, 256), BF16),
                dma((GROUPS,)),
                dma((2,)),
                dma((2,)),
                dma((1,)),
                dma((2, 2)),
                dma((2, 2)),
                dma((3, 7)),
                dma((3, 7)),
                dma((4, 2)),
                dma((4, 2)),
            ],
            compiler_params=pltpu.CompilerParams(
                collective_id=0, has_side_effects=True, vmem_limit_bytes=56 * 1024 * 1024
            ),
        )(rows_of(launch), rows_of(cotangent), filter_taps, offsets)
        return field_of(arrival), field_of(gradient)

    placed = (P("chan", None, None, "tm"), P("chan", None, None, "tm"), P(), P(None, "chan"))
    return jax.shard_map(
        local,
        mesh=mesh,
        in_specs=placed,
        out_specs=(P("chan", None, None, "tm"), P("chan", None, None, "tm")),
        check_vma=False,
    )
```

```python
import functools

import jax
import jax.numpy as jnp
from jax import lax
from jax.experimental import pallas as pl
from jax.experimental.pallas import tpu as pltpu
from jax.sharding import PartitionSpec as P

NONLINEAR = 0.001953125
ROWS = 64
HALF = 64
GROUPS = 4
PLANES = 32 // GROUPS
CHANS = 16
MESH = pl.DeviceIdType.MESH
F32 = jnp.float32
BF16 = jnp.bfloat16


def sincos(x):
    k = jnp.floor(x * 0.6366197723675814 + 0.5)
    r = x - k * 1.5703125
    r = r - k * 4.837512969970703125e-4
    r = r - k * 7.549789948768648e-8
    n = k.astype(jnp.int32)
    r2 = r * r
    s = r + r * r2 * (-1.6666654611e-1 + r2 * (8.3321608736e-3 - r2 * 1.9515295891e-4))
    c = 1.0 - 0.5 * r2 + r2 * r2 * (4.166664568298827e-2 + r2 * (2.443315711809948e-5 * r2 - 1.388731625493765e-3))
    swap = (n & 1) == 1
    sine = jnp.where(swap, c, s)
    cosine = jnp.where(swap, s, c)
    sine = jnp.where((n & 2) == 2, -sine, sine)
    cosine = jnp.where(((n + 1) & 2) == 2, -cosine, cosine)
    return cosine, sine


def split(x):
    high = x.astype(BF16)
    low = (x - high.astype(F32)).astype(BF16)
    return high, low


def plane(index, pitch, first):
    return pl.ds(pl.multiple_of(index * pitch, 8) + first, ROWS)


def build_tables(taps, forward, backward):
    row = lax.broadcasted_iota(jnp.int32, (128, 128), 0)
    col = lax.broadcasted_iota(jnp.int32, (128, 128), 1)
    lag = col - row
    mats = []
    for comp in range(2):
        body = jnp.broadcast_to(taps[comp : comp + 1, 0:128], (128, 128))
        last = jnp.broadcast_to(taps[comp : comp + 1, 128:129], (128, 128))
        minus = pltpu.roll(body, HALF, 1)
        plus = jnp.where(col == HALF, last, minus)
        minus = pltpu.roll(minus, 0, 1, stride=1, stride_axis=0)
        plus = pltpu.roll(plus, 0, 1, stride=1, stride_axis=0)
        centre = jnp.where(lag == -HALF, minus, plus)
        centre = jnp.where((lag >= -HALF) & (lag <= HALF), centre, 0.0)
        rim = jnp.where(lag == HALF, minus, plus)
        rim = jnp.where((lag <= -HALF) | (lag >= HALF), rim, 0.0)
        mats.append((centre, rim))
    for table, adjoint in ((forward, False), (backward, True)):
        for part in range(2):
            real, imag = mats[0][part], mats[1][part]
            if adjoint:
                real, imag = real.T, -imag.T
            for place, block in ((0, (real, imag)), (1, (-imag, real))):
                start = part * 256 + place * 128
                for side in range(2):
                    high, low = split(block[side])
                    cols = slice(side * 128, side * 128 + 128)
                    table[start : start + 128, cols] = high
                    table[512 + start : 512 + start + 128, cols] = high
                    table[1024 + start : 1024 + start + 128, cols] = low


def kernel(n, launch, cot, taps, off, arr, grad, X, S, D1, D2, CA1, SA1, CP1, SP1, CP2, SP2, C, R, W, LHA, LHB, PP, ZR, ZI, TH, TE,
           OWN, RXA, RXF, RXM, RXD, HS, TT, ES, ER, XE, EV, OC, TF, TB, load_sem, edge_ss, edge_rs,
           cot_sem, cot_ss, cot_rs, tx_ss, rx_rs, w_ss, w_rs):
    tm, chan = lax.axis_index("tm"), lax.axis_index("chan")
    nxt, prv = lax.rem(tm + 1, n), lax.rem(tm + n - 1, n)
    core = lax.rem(chan, 2)
    sib = chan + 1 - 2 * core
    far = lax.rem(chan + 2, 4)
    far_sib = lax.rem(sib + 2, 4)
    side_tm = core * nxt + (1 - core) * prv

    def launch_load(g):
        return pltpu.make_async_copy(
            launch.at[pl.ds(PLANES * g, PLANES)], X.at[pl.ds(PLANES * g, PLANES), pl.ds(8, 128)], load_sem.at[g]
        )

    for g in range(GROUPS):
        launch_load(g).start()
    barrier = pltpu.get_barrier_semaphore()
    peers = [(tm, sib), (tm, far), (nxt, chan), (prv, chan), (side_tm, sib), (side_tm, far_sib)]
    for peer in peers:
        pl.semaphore_signal(barrier, inc=1, device_id=peer, device_id_type=MESH)
    cot_copy = pltpu.make_async_copy(cot, C.at[:, pl.ds(32, 128)], cot_sem.at[0])
    cot_copy.start()

    def send(src, dst, ss, rs, peer):
        copy = pltpu.make_async_remote_copy(
            src_ref=src, dst_ref=dst, send_sem=ss, recv_sem=rs, device_id=peer, device_id_type=MESH
        )
        copy.start()
        return copy

    def move_cot(half):
        cps = pl.ds(16 * half, 16)
        return [
            send(cot.at[cps, pl.ds(96, 32)], C.at[cps, pl.ds(0, 32)], cot_ss.at[half, 0], cot_rs.at[half, 0],
                 (nxt, chan)),
            send(cot.at[cps, pl.ds(0, 32)], C.at[cps, pl.ds(160, 32)], cot_ss.at[half, 1], cot_rs.at[half, 1],
                 (prv, chan)),
        ]

    build_tables(taps, TF, TB)
    for buffer in (PP, ZR, ZI):
        for c in range(CHANS):
            buffer[c * 144 : c * 144 + 40] = jnp.zeros((40, 128), F32)
            buffer[c * 144 + 104 : c * 144 + 144] = jnp.zeros((40, 128), F32)
    X[:, 0:8] = jnp.zeros((32, 8, 128), F32)
    X[:, 136:144] = jnp.zeros((32, 8, 128), F32)
    lane = lax.broadcasted_iota(jnp.int32, (ROWS, 128), 1)
    short = lax.broadcasted_iota(jnp.int32, (32, 128), 1)

    def apply_filter(load, table, finish, first=0, before=None, count=16):
        def prepare(g, LH):
            for j in range(count):
                for comp in range(2):
                    x = load(count * g + j, comp, 0)
                    z = jnp.where(lane < HALF, load(count * g + j, comp, 1), load(count * g + j, comp, -1))
                    for place, value in ((comp, x), (2 + comp, z)):
                        high, low = split(value)
                        LH[j * ROWS : j * ROWS + ROWS, place * 128 : place * 128 + 128] = high
                        LH[j * ROWS : j * ROWS + ROWS, 512 + place * 128 : 640 + place * 128] = low

        def multiply(LH):
            used = count * ROWS
            out = jnp.dot(LH[0:used], table[0:1024], preferred_element_type=F32)
            return out + jnp.dot(LH[0:used, 0:512], table[1024:1536], preferred_element_type=F32)

        def complete(g, out):
            for a in range(count // 2):
                values = []
                for pol in range(2):
                    start = (2 * a + pol) * ROWS
                    values.append((out[start : start + ROWS, 0:128], out[start : start + ROWS, 128:256]))
                finish(count // 2 * g + a, values)

        if before is not None:
            before(first)
        prepare(first, LHA)
        if before is not None:
            before(first + 1)
        out = multiply(LHA)
        prepare(first + 1, LHB)
        complete(first, out)
        complete(first + 1, multiply(LHB))

    def shift_of(step, c):
        total = off[0, c]
        return total + off[1, c] if step else total

    def sizes(step):
        reach = 8 * (step + 1)
        margin = reach + 8
        ext = ROWS + 2 * margin
        return margin, ext, ext // 2, margin + reach

    def exchange_begin(k, step, sources):
        margin, ext, half, count = sizes(step)
        for a, source in enumerate(sources):
            def add(c, acc, source=source):
                start = pl.multiple_of(c * 144, 8) + 40 - margin - shift_of(step, c)
                return acc + source[pl.ds(start, ext), :]

            OWN[k, a, 0:ext] = lax.fori_loop(0, CHANS, add, jnp.zeros((ext, 128), F32), unroll=4)
        arrays = len(sources)
        theirs = pl.ds(pl.multiple_of((1 - core) * half, 8), half)
        return [
            send(OWN.at[k, pl.ds(0, arrays), theirs], RXA.at[k, pl.ds(0, arrays), pl.ds(0, half)],
                 tx_ss.at[k, 0], rx_rs.at[k, 0], (tm, sib))
        ]

    def exchange_middle(k, step, copies, arrays, fields):
        margin, ext, half, count = sizes(step)
        for e, field in enumerate(fields):
            for side, row in ((0, ROWS - 1), (1, 0)):
                one = field[pl.ds(row, 32, stride=2 * ROWS), :]
                two = field[pl.ds(ROWS + row, 32, stride=2 * ROWS), :]
                if side == 0:
                    one = pltpu.roll(one, HALF, 1)
                else:
                    two = pltpu.roll(two, HALF, 1)
                ES[k, e, side] = jnp.where(short < HALF, one, two)
        copies[0].wait_recv()
        mine = pl.ds(pl.multiple_of(core * half, 8), half)
        for a in range(arrays):
            HS[k, a, 0:half] = OWN[k, a, mine, :] + RXA[k, a, 0:half]
        every = pl.ds(0, arrays)
        start = pl.multiple_of(core * (64 - half) + (1 - core) * 8, 8)
        rim = HS.at[k, every, pl.ds(start, count)]
        copies.append(send(rim, RXD.at[k, every, pl.ds(0, count)], tx_ss.at[k, 1], rx_rs.at[k, 1], (side_tm, far_sib)))
        copies.append(send(rim, RXM.at[k, every, pl.ds(0, count)], tx_ss.at[k, 2], rx_rs.at[k, 2], (side_tm, sib)))
        copies.append(
            send(HS.at[k, every, pl.ds(0, half)], RXF.at[k, every, pl.ds(0, half)], tx_ss.at[k, 3], rx_rs.at[k, 3],
                 (tm, far))
        )
        several = pl.ds(0, len(fields))
        copies.append(send(ES.at[k, several, 0], ER.at[k, several, 0], tx_ss.at[k, 5], rx_rs.at[k, 5], (nxt, chan)))
        copies.append(send(ES.at[k, several, 1], ER.at[k, several, 1], tx_ss.at[k, 6], rx_rs.at[k, 6], (prv, chan)))

    def exchange_end(k, step, copies, arrays):
        margin, ext, half, count = sizes(step)
        for copy in copies[1:4]:
            copy.wait_recv()
        base = pl.multiple_of(core * half, 8)
        rim = pl.multiple_of(core * half + core * (half - count), 8)
        for a in range(arrays):
            TT[k, a, pl.ds(base, half), :] = HS[k, a, 0:half] + RXF[k, a, 0:half]
            TT[k, a, pl.ds(rim, count), :] = TT[k, a, pl.ds(rim, count), :] + RXM[k, a, 0:count] + RXD[k, a, 0:count]
        block = TT.at[k, pl.ds(0, arrays), pl.ds(base, half)]
        last = send(block, block, tx_ss.at[k, 4], rx_rs.at[k, 4], (tm, sib))
        last.wait()
        copies[0].wait_send()
        for copy in copies[1:4]:
            copy.wait_send()
        for copy in copies[4:]:
            copy.wait()

    def edge_rows(k, a, source, step):
        margin = sizes(step)[0]
        for c in range(CHANS):
            start = margin + shift_of(step, c)
            TE[k, a, 0, c : c + 1] = source[pl.ds(start - 1, 1), :]
            TE[k, a, 1, c : c + 1] = source[pl.ds(start + ROWS, 1), :]

    def edge_planes(k, e, side):
        planes = []
        for q in range(4):
            both = ER.at[k, e, side][pl.ds(q // 2, CHANS, stride=2), :]
            planes.append(pltpu.roll(both, HALF, 1) if q % 2 == side else both)
        return planes

    def put_edge(side, planes):
        row = 7 if side == 0 else 72
        for q in range(4):
            S[pl.ds(q * 80 + row, CHANS, stride=320), :] = planes[q]

    def load_x(cp, comp, d):
        return X[cp, pl.ds(8 + 2 * d + comp, ROWS, stride=2), :]

    def load_s(cp, comp, d):
        return S[plane(2 * cp + comp, 80, 8 + d), :]

    def field(ref, c, q):
        return ref[plane(4 * c + q, ROWS, 0), :]

    def rows(ref, c):
        return ref[plane(c, ROWS, 0), :]

    def middle(ref, c):
        return ref[plane(c, 144, 40), :]

    def keep_1(c, values):
        power = jnp.zeros((ROWS, 128), F32)
        for pol in range(2):
            re, im = values[pol]
            D1[plane(4 * c + 2 * pol, ROWS, 0), :] = re
            D1[plane(4 * c + 2 * pol + 1, ROWS, 0), :] = im
            power = power + re * re + im * im
        PP[plane(c, 144, 40), :] = power
        ca, sa = sincos(NONLINEAR * power)
        CA1[plane(c, ROWS, 0), :] = ca
        SA1[plane(c, ROWS, 0), :] = sa

    def wait_load(g):
        launch_load(g).wait()

    apply_filter(load_x, TF, keep_1, 0, wait_load, PLANES)
    pl.semaphore_wait(barrier, len(peers))
    edge_copies = [
        send(launch.at[:, pl.ds(120, 8)], XE.at[0], edge_ss.at[0], edge_rs.at[0], (nxt, chan)),
        send(launch.at[:, pl.ds(0, 8)], XE.at[1], edge_ss.at[1], edge_rs.at[1], (prv, chan)),
    ]
    cot_copies = move_cot(0)
    apply_filter(load_x, TF, keep_1, 2, wait_load, PLANES)
    for copy in edge_copies:
        copy.wait()
    for cp in range(32):
        EV[0, 2 * cp : 2 * cp + 2] = XE[0, cp, 6:8]
        EV[1, 2 * cp : 2 * cp + 2] = XE[1, cp, 0:2]
    pieces = []
    for side in range(2):
        inside = short >= HALF if side == 0 else short < HALF
        parts = [jnp.where(inside, EV.at[side][pl.ds(comp, 32, stride=2), :], 0.0) for comp in range(2)]
        high, low = split(jnp.concatenate(parts, axis=1))
        pieces.append(jnp.concatenate([high, low, high], axis=1))
    rim_table = jnp.concatenate([TF[256:512], TF[768:1024], TF[1280:1536]], axis=0)
    added = jnp.dot(jnp.concatenate(pieces, axis=0), rim_table, preferred_element_type=F32)
    OC[0] = added[:, 0:128]
    OC[1] = added[:, 128:256]
    for side in range(2):
        row = 0 if side == 0 else ROWS - 1
        power = jnp.zeros((CHANS, 128), F32)
        for q in range(4):
            place = pl.ds(q * ROWS + row, CHANS, stride=4 * ROWS)
            value = D1[place, :] + OC.at[q % 2][pl.ds(32 * side + q // 2, CHANS, stride=2), :]
            D1[place, :] = value
            power = power + value * value
        PP[pl.ds(40 + row, CHANS, stride=144), :] = power
        ca, sa = sincos(NONLINEAR * power)
        CA1[pl.ds(row, CHANS, stride=ROWS), :] = ca
        SA1[pl.ds(row, CHANS, stride=ROWS), :] = sa

    copies = exchange_begin(0, 0, [PP])
    exchange_middle(0, 0, copies, 1, [D1])
    cot_copies += move_cot(1)
    exchange_end(0, 0, copies, 1)

    def turn(k):
        ext = sizes(k)[1]
        ct, st = sincos(2.0 * NONLINEAR * TT[k, 0, 0:ext])
        TH[k, 0, 0:ext] = ct
        TH[k, 1, 0:ext] = st

    turn(0)
    edge_rows(0, 0, TH.at[0, 0], 0)
    edge_rows(0, 1, TH.at[0, 1], 0)

    def rotate_1(c, carry):
        start = pl.ds(16 + shift_of(0, c), ROWS)
        ct, st = TH[0, 0, start, :], TH[0, 1, start, :]
        ca, sa = rows(CA1, c), rows(SA1, c)
        cs, sn = ct * ca + st * sa, st * ca - ct * sa
        CP1[plane(c, ROWS, 0), :] = cs
        SP1[plane(c, ROWS, 0), :] = sn
        for pol in range(2):
            re, im = field(D1, c, 2 * pol), field(D1, c, 2 * pol + 1)
            S[plane(4 * c + 2 * pol, 80, 8), :] = re * cs - im * sn
            S[plane(4 * c + 2 * pol + 1, 80, 8), :] = re * sn + im * cs
        return carry

    lax.fori_loop(0, CHANS, rotate_1, 0)
    for side in range(2):
        e = edge_planes(0, 0, side)
        ca, sa = sincos(NONLINEAR * (e[0] * e[0] + e[1] * e[1] + e[2] * e[2] + e[3] * e[3]))
        ct, st = TE[0, 0, side], TE[0, 1, side]
        cs, sn = ct * ca + st * sa, st * ca - ct * sa
        put_edge(side, [e[0] * cs - e[1] * sn, e[0] * sn + e[1] * cs, e[2] * cs - e[3] * sn, e[2] * sn + e[3] * cs])

    def keep_2(c, values):
        power = jnp.zeros((ROWS, 128), F32)
        for pol in range(2):
            re, im = values[pol]
            power = power + re * re + im * im
        PP[plane(c, 144, 40), :] = power
        ca, sa = sincos(NONLINEAR * power)
        CP2[plane(c, ROWS, 0), :] = ca
        SP2[plane(c, ROWS, 0), :] = sa
        for pol in range(2):
            re, im = values[pol]
            D2[plane(4 * c + 2 * pol, ROWS, 0), :] = re
            D2[plane(4 * c + 2 * pol + 1, ROWS, 0), :] = im
            W[4 * c + 2 * pol, 16:80] = re * ca + im * sa
            W[4 * c + 2 * pol + 1, 16:80] = im * ca - re * sa

    apply_filter(load_s, TF, keep_2)
    cot_copy.wait()
    for copy in cot_copies:
        copy.wait()

    def project_2(c, carry):
        shift = shift_of(1, c)
        ca, sa = rows(CP2, c), rows(SP2, c)
        zr, zi = jnp.zeros((ROWS, 128), F32), jnp.zeros((ROWS, 128), F32)
        for pol in range(2):
            re, im = field(D2, c, 2 * pol), field(D2, c, 2 * pol + 1)
            gr = C[2 * c + pol, pl.ds(32 + 2 * shift, ROWS, stride=2), :]
            gi = C[2 * c + pol, pl.ds(33 + 2 * shift, ROWS, stride=2), :]
            hr = gr * ca - gi * sa
            hi = gr * sa + gi * ca
            R[plane(4 * c + 2 * pol, ROWS, 0), :] = hr
            R[plane(4 * c + 2 * pol + 1, ROWS, 0), :] = hi
            zr = zr + hr * re + hi * im
            zi = zi + hi * re - hr * im
        ZR[plane(c, 144, 40), :] = zr
        ZI[plane(c, 144, 40), :] = zi
        return carry

    lax.fori_loop(0, CHANS, project_2, 0)
    copies = exchange_begin(1, 1, [PP, ZR, ZI])
    exchange_middle(1, 1, copies, 3, [D2, R])
    def move_arrival(part, start, size):
        planes = pl.ds(start, size)
        return [
            send(W.at[planes, pl.ds(64, 16)], W.at[planes, pl.ds(0, 16)], w_ss.at[part, 0], w_rs.at[part, 0],
                 (nxt, chan)),
            send(W.at[planes, pl.ds(16, 16)], W.at[planes, pl.ds(80, 16)], w_ss.at[part, 1], w_rs.at[part, 1],
                 (prv, chan)),
        ]

    w_copies = move_arrival(0, 0, 16)
    exchange_end(1, 1, copies, 3)
    w_copies += move_arrival(2, 16, 32)
    turn(1)
    TT[1, 0] = TT[1, 2] * TH[1, 0] - TT[1, 1] * TH[1, 1]
    edge_rows(1, 0, TH.at[1, 0], 1)
    edge_rows(1, 1, TH.at[1, 1], 1)
    edge_rows(1, 2, TT.at[1, 0], 1)

    def weigh_2(c, carry):
        start = pl.ds(24 + shift_of(1, c), ROWS)
        ct, st, total = TH[1, 0, start, :], TH[1, 1, start, :], TT[1, 0, start, :]
        own = middle(ZI, c) * ct - middle(ZR, c) * st
        w = 2.0 * NONLINEAR * (2.0 * total - own)
        for pol in range(2):
            rr, ri = field(R, c, 2 * pol), field(R, c, 2 * pol + 1)
            S[plane(4 * c + 2 * pol, 80, 8), :] = rr * ct + ri * st + w * field(D2, c, 2 * pol)
            S[plane(4 * c + 2 * pol + 1, 80, 8), :] = ri * ct - rr * st + w * field(D2, c, 2 * pol + 1)
        return carry

    lax.fori_loop(0, CHANS, weigh_2, 0)
    for side in range(2):
        d, r = edge_planes(1, 0, side), edge_planes(1, 1, side)
        ct, st = TE[1, 0, side], TE[1, 1, side]
        rr = [r[0] * ct + r[1] * st, r[1] * ct - r[0] * st, r[2] * ct + r[3] * st, r[3] * ct - r[2] * st]
        own = rr[1] * d[0] - rr[0] * d[1] + rr[3] * d[2] - rr[2] * d[3]
        w = 2.0 * NONLINEAR * (2.0 * TE[1, 2, side] - own)
        put_edge(side, [rr[q] + w * d[q] for q in range(4)])

    def back_rotate(c, values):
        cs, sn = rows(CP1, c), rows(SP1, c)
        own = jnp.zeros((ROWS, 128), F32)
        for pol in range(2):
            re, im = values[pol]
            rr = re * cs + im * sn
            ri = im * cs - re * sn
            R[plane(4 * c + 2 * pol, ROWS, 0), :] = rr
            R[plane(4 * c + 2 * pol + 1, ROWS, 0), :] = ri
            own = own + ri * field(D1, c, 2 * pol) - rr * field(D1, c, 2 * pol + 1)
        PP[plane(c, 144, 40), :] = own

    apply_filter(load_s, TB, back_rotate)
    copies = exchange_begin(2, 0, [PP])
    exchange_middle(2, 0, copies, 1, [R])
    w_copies += move_arrival(1, 48, 16)
    exchange_end(2, 0, copies, 1)
    edge_rows(2, 0, TT.at[2, 0], 0)

    def weigh_1(c, carry):
        total = TT[2, 0, pl.ds(16 + shift_of(0, c), ROWS), :]
        w = 2.0 * NONLINEAR * (2.0 * total - middle(PP, c))
        for q in range(4):
            S[plane(4 * c + q, 80, 8), :] = field(R, c, q) + w * field(D1, c, q)
        return carry

    lax.fori_loop(0, CHANS, weigh_1, 0)
    for side in range(2):
        r, d = edge_planes(2, 0, side), edge_planes(0, 0, side)
        own = r[1] * d[0] - r[0] * d[1] + r[3] * d[2] - r[2] * d[3]
        w = 2.0 * NONLINEAR * (2.0 * TE[2, 0, side] - own)
        put_edge(side, [r[q] + w * d[q] for q in range(4)])

    def put_results(c, values):
        for pol in range(2):
            for comp in range(2):
                grad[2 * c + pol, pl.ds(comp, ROWS, stride=2), :] = values[pol][comp]

    apply_filter(load_s, TB, put_results)
    for copy in w_copies:
        copy.wait()

    def put_arrival(c, carry):
        start = pl.ds(16 - shift_of(1, c), ROWS)
        ct, st = TH[1, 0, 24:88], TH[1, 1, 24:88]
        for pol in range(2):
            re, im = W[4 * c + 2 * pol, start, :], W[4 * c + 2 * pol + 1, start, :]
            arr[2 * c + pol, pl.ds(0, ROWS, stride=2), :] = re * ct - im * st
            arr[2 * c + pol, pl.ds(1, ROWS, stride=2), :] = re * st + im * ct
        return carry

    lax.fori_loop(0, CHANS, put_arrival, 0, unroll=2)


def rows_of(x):
    return x.reshape(32, 2, ROWS, 128).transpose(0, 2, 1, 3).reshape(32, 2 * ROWS, 128)


def field_of(x):
    return x.reshape(32, ROWS, 2, 128).transpose(0, 2, 1, 3).reshape(16, 2, 2, ROWS * 128)


def solution(mesh):
    n = mesh.shape["tm"]

    def local(launch, cotangent, filter_taps, offsets):
        out = jax.ShapeDtypeStruct((32, 2 * ROWS, 128), F32)
        anywhere = pl.BlockSpec(memory_space=pl.ANY)
        dma = pltpu.SemaphoreType.DMA
        arrival, gradient = pl.pallas_call(
            functools.partial(kernel, n),
            out_shape=(pltpu.VMEM((32, 2 * ROWS, 128), F32), pltpu.VMEM((32, 2 * ROWS, 128), F32)),
            in_specs=[
                anywhere,
                anywhere,
                pl.BlockSpec(memory_space=pltpu.VMEM),
                pl.BlockSpec(memory_space=pltpu.SMEM),
            ],
            out_specs=(pl.BlockSpec(memory_space=pltpu.VMEM), pl.BlockSpec(memory_space=pltpu.VMEM)),
            scratch_shapes=[
                pltpu.VMEM((32, 144, 128), F32),
                pltpu.VMEM((64 * 80, 128), F32),
                pltpu.VMEM((64 * ROWS, 128), F32),
                pltpu.VMEM((64 * ROWS, 128), F32),
                pltpu.VMEM((CHANS * ROWS, 128), F32),
                pltpu.VMEM((CHANS * ROWS, 128), F32),
                pltpu.VMEM((CHANS * ROWS, 128), F32),
                pltpu.VMEM((CHANS * ROWS, 128), F32),
                pltpu.VMEM((CHANS * ROWS, 128), F32),
                pltpu.VMEM((CHANS * ROWS, 128), F32),
                pltpu.VMEM((32, 192, 128), F32),
                pltpu.VMEM((64 * ROWS, 128), F32),
                pltpu.VMEM((64, 96, 128), F32),
                pltpu.VMEM((16 * ROWS, 1024), BF16),
                pltpu.VMEM((16 * ROWS, 1024), BF16),
                pltpu.VMEM((CHANS * 144, 128), F32),
                pltpu.VMEM((CHANS * 144, 128), F32),
                pltpu.VMEM((CHANS * 144, 128), F32),
                pltpu.VMEM((2, 2, 112, 128), F32),
                pltpu.VMEM((3, 3, 2, CHANS, 128), F32),
                pltpu.VMEM((3, 3, 112, 128), F32),
                pltpu.VMEM((3, 3, 56, 128), F32),
                pltpu.VMEM((3, 3, 56, 128), F32),
                pltpu.VMEM((3, 3, 40, 128), F32),
                pltpu.VMEM((3, 3, 40, 128), F32),
                pltpu.VMEM((3, 3, 56, 128), F32),
                pltpu.VMEM((3, 3, 112, 128), F32),
                pltpu.VMEM((3, 2, 2, 32, 128), F32),
                pltpu.VMEM((3, 2, 2, 32, 128), F32),
                pltpu.VMEM((2, 32, 8, 128), F32),
                pltpu.VMEM((2, 64, 128), F32),
                pltpu.VMEM((2, 64, 128), F32),
                pltpu.VMEM((1536, 256), BF16),
                pltpu.VMEM((1536, 256), BF16),
                dma((GROUPS,)),
                dma((2,)),
                dma((2,)),
                dma((1,)),
                dma((2, 2)),
                dma((2, 2)),
                dma((3, 7)),
                dma((3, 7)),
                dma((4, 2)),
                dma((4, 2)),
            ],
            compiler_params=pltpu.CompilerParams(
                collective_id=0, has_side_effects=True, vmem_limit_bytes=56 * 1024 * 1024
            ),
        )(rows_of(launch), rows_of(cotangent), filter_taps, offsets)
        return field_of(arrival), field_of(gradient)

    placed = (P("chan", None, None, "tm"), P("chan", None, None, "tm"), P(), P(None, "chan"))
    return jax.shard_map(
        local,
        mesh=mesh,
        in_specs=placed,
        out_specs=(P("chan", None, None, "tm"), P("chan", None, None, "tm")),
        check_vma=False,
    )
```
